256 devices in a mesh: domain: 128 (over z, x, y_lo, core), band: 2 (over y_hi).
Axes of the slice: x: 4, y: 4 (y_hi: 2, y_lo: 2; y = y_hi * 2 + y_lo), z: 8, core: 2. Of those that a mesh axis runs over, the one named last changes fastest.
Arguments:
- orbitals: float32 [64, 262144], P('band', 'domain'), may hold values from -6 to 6
- others: float32 [192, 262144], P('band', 'domain'), may hold values from -6 to 6
- potential: float32 [262144], P('domain'), may hold values from -8 to 8
- cell_scale: float32 [98304], P('domain'), may hold values from 0.5 to 2
- connectivity: int32 [64, 98304], P(None, 'domain'), may hold values from 0 to 5119, as said below
- send_up: int32 [196608], P('domain'), may hold values from 0 to 2047, as said below
- send_down: int32 [196608], P('domain'), may hold values from 0 to 2047, as said below
- stiffness: float32 [64, 64], replicated, may hold values from -0.25 to 3, as said below
- rotation: float32 [256, 256], replicated, may hold values from -0.375 to 0.375
Outputs:
- rotated: float32 [256, 262144], P('band', 'domain')
The draws below stay inside these ranges and needn't reach their ends.
Inputs may be any that keep to these rules, and one draw needn't show every extreme that they name: `connectivity`: positions of a slab's extended node list: the first 1536 are the previous slab's shared nodes in the order of its send_up list, the next 2048 the slab's own nodes, the last 1536 the next slab's shared nodes in the order of its send_down list. The nodes of the cell numbered j within its slab lie among the 256 consecutive positions that begin at j * 4864 // 767. Within a slab, cells numbered below 288 have all nodes among the first 2560 positions and the others none among the first 1536; cells numbered 768 - 288 or more have all nodes among the last 2560 positions and the others none among the last 1536. `send_up`: for each slab in turn, 1536 distinct node numbers within that slab. `send_down`: for each slab in turn, 1536 distinct node numbers within that slab. `stiffness`: Symmetric.
All inputs are finite; a program needn't handle non-finite values.
Results may differ from the reference program's by a relative error of at most 0.0001.
Values sent between devices are 32-bit elements; how exact they have to be, the bound alone decides.
A program may use at most 64 MiB of HBM per device.

```python
import math
import jax
import jax.numpy as jnp
from jax import lax

NODE_DEV = 2048
NPC = 64
FILT = 64
PANEL = 256
DEGREES = 2
WINDOW = 256
CELLS_DEV = 768
RIM = 1536
NODES = 262144
CELLS = 98304
N_DOMAIN = 128


def draw_connectivity(key, part):
    cell_total = CELLS_DEV * N_DOMAIN
    ext_len = NODE_DEV + 2 * RIM
    local_cell = jnp.arange(cell_total, dtype=jnp.int32) % CELLS_DEV
    window_start = local_cell * (ext_len - WINDOW) // (CELLS_DEV - 1)
    offsets = jax.random.randint(key, (NPC, cell_total), 0, WINDOW, dtype=jnp.int32)
    node_ids = window_start[None, :] + offsets
    slot_index = jnp.arange(NPC, dtype=jnp.int32)[:, None]
    first_slot = (local_cell == 0)[None, :] & (slot_index == 0)
    last_slot = (local_cell == CELLS_DEV - 1)[None, :] & (slot_index == NPC - 1)
    node_ids = jnp.where(first_slot, 0, jnp.where(last_slot, ext_len - 1, node_ids))
    return node_ids.astype(jnp.int32)


def boundary_list(key):

    def one_slab(slab_index):
        slab_key = jax.random.fold_in(key, slab_index)
        inner = jax.random.permutation(jax.random.fold_in(slab_key, 1), NODE_DEV - 2) + 1
        chosen = jnp.concatenate([jnp.array([0, NODE_DEV - 1], dtype=jnp.int32), inner[:RIM - 2].astype(jnp.int32)])
        shuffle = jax.random.permutation(jax.random.fold_in(slab_key, 2), RIM)
        return chosen[shuffle]
    lists = jax.vmap(one_slab)(jnp.arange(N_DOMAIN, dtype=jnp.int32))
    return lists.reshape(-1).astype(jnp.int32)


def draw_send_up(key, part):
    return boundary_list(jax.random.fold_in(key, 11))


def draw_send_down(key, part):
    return boundary_list(jax.random.fold_in(key, 23))


def draw_stiffness(key, part):
    key_off, key_diag = jax.random.split(jax.random.fold_in(key, 37))
    raw_draw = jax.random.uniform(key_off, (NPC, NPC), jnp.float32, -1.0, 1.0)
    off_diag = 0.125 * (raw_draw + raw_draw.T)
    diagonal_entries = jax.random.uniform(key_diag, (NPC,), jnp.float32, 2.0, 3.0)
    on_diagonal = jnp.eye(NPC, dtype=bool)
    return jnp.where(on_diagonal, diagonal_entries[:, None], off_diag).astype(jnp.float32)


def levels(stream_key, shape, cuts, smallest, top_value):
    loudness, own = 1.0, jax.random.fold_in(stream_key, 6)
    for dim, parts in cuts:
        heights = jnp.exp(jax.random.uniform(jax.random.fold_in(own, dim), (parts,), jnp.float32, smallest / len(cuts), top_value / len(cuts)))
        loudness = loudness * jnp.repeat(heights, shape[dim] // parts).reshape([-1 if axis == dim else 1 for axis in range(len(shape))])
    return loudness


def normal_values(own_key, dims, width, reach, shards=(), kind=jnp.bfloat16):
    level = levels(own_key, dims, shards, -0.22, 0.18) if shards else 1.0
    drawn = jax.random.normal(own_key, dims, jnp.float32) * width * level
    return jnp.minimum(jnp.maximum(drawn, -reach), reach).astype(kind)


def setup_inputs(seed: int = 0) -> dict:
    keys = jax.random.split(jax.random.key(seed), 10)
    orbitals = normal_values(keys[0], (FILT, NODES), 1.0, 6.0, ((0, 2), (1, 128)), jnp.float32)
    others = normal_values(keys[1], (PANEL - FILT, NODES), 1.0, 6.0, ((0, 2), (1, 128)), jnp.float32)
    potential = jnp.clip(jax.random.uniform(keys[2], (NODES,), jnp.float32, -8.0, 8.0) * levels(keys[2], (NODES,), ((0, 128),), -0.4, 0.0), -8.0, 8.0)
    cell_scale = jnp.clip(jnp.exp(math.log(2.0) - 1.3862944 * jax.random.uniform(keys[3], (CELLS,), jnp.float32) ** levels(keys[3], (CELLS,), ((0, 128),), -0.2, 0.2)), 0.5, 2.0)
    connectivity = draw_connectivity(jax.random.fold_in(keys[9], 71), 0)
    send_up = draw_send_up(jax.random.fold_in(keys[9], 71), 0)
    send_down = draw_send_down(jax.random.fold_in(keys[9], 71), 0)
    stiffness = draw_stiffness(jax.random.fold_in(keys[9], 71), 0)
    rotation = normal_values(keys[8], (PANEL, PANEL), PANEL ** -0.5, 0.375, (), jnp.float32)
    return dict(orbitals=orbitals, others=others, potential=potential, cell_scale=cell_scale, connectivity=connectivity, send_up=send_up, send_down=send_down, stiffness=stiffness, rotation=rotation)


FILTER_CENTER = 64.0
FILTER_HALF = 64.0


def node_numbers(connectivity, send_up, send_down):
    cell_total = connectivity.shape[1]
    slab_index = (jnp.arange(cell_total, dtype=jnp.int32) // CELLS_DEV)[None, :]
    below_slab = (slab_index - 1) % N_DOMAIN
    above_slab = (slab_index + 1) % N_DOMAIN
    up_table = send_up.reshape(N_DOMAIN, RIM)
    down_table = send_down.reshape(N_DOMAIN, RIM)
    lower_node = below_slab * NODE_DEV + up_table[below_slab, jnp.clip(connectivity, 0, RIM - 1)]
    own_node = slab_index * NODE_DEV + jnp.clip(connectivity - RIM, 0, NODE_DEV - 1)
    upper_node = above_slab * NODE_DEV + down_table[above_slab, jnp.clip(connectivity - RIM - NODE_DEV, 0, RIM - 1)]
    inside = jnp.where(connectivity < RIM + NODE_DEV, own_node, upper_node)
    return jnp.where(connectivity < RIM, lower_node, inside).astype(jnp.int32)


def operate(vectors, node_of, potential, cell_scale, stiffness):
    def one_slab(slab_index, running):
        node_cols = lax.dynamic_slice_in_dim(node_of, slab_index * CELLS_DEV, CELLS_DEV, 1)
        scale_rows = lax.dynamic_slice_in_dim(cell_scale, slab_index * CELLS_DEV, CELLS_DEV, 0)
        values = vectors[:, node_cols]
        images = jnp.einsum("ij,ojc->oic", stiffness, values, precision=lax.Precision.HIGHEST) * scale_rows
        return running.at[:, node_cols].add(images)

    running = lax.fori_loop(0, N_DOMAIN, one_slab, jnp.zeros_like(vectors))
    return running + potential * vectors


def reference(orbitals, others, potential, cell_scale, connectivity, send_up, send_down, stiffness, rotation):
    node_of = node_numbers(connectivity, send_up, send_down)
    previous = orbitals
    current = (operate(orbitals, node_of, potential, cell_scale, stiffness) - FILTER_CENTER * orbitals) / FILTER_HALF
    for degree in range(DEGREES - 1):
        image = operate(current, node_of, potential, cell_scale, stiffness)
        following = 2.0 * (image - FILTER_CENTER * current) / FILTER_HALF - previous
        previous = current
        current = following
    block_part = jnp.dot(rotation[:FILT].T, current, precision=lax.Precision.HIGHEST, preferred_element_type=jnp.float32)
    other_part = jnp.dot(rotation[FILT:].T, others, precision=lax.Precision.HIGHEST, preferred_element_type=jnp.float32)
    return block_part + other_part
```

```python
import functools

import jax
import jax.numpy as jnp
from jax import lax
from jax.experimental import pallas as pl
from jax.experimental.pallas import tpu as pltpu
from jax.sharding import PartitionSpec as P

bf16 = jnp.bfloat16
f32 = jnp.float32
MESH = pl.DeviceIdType.MESH

WINDOW = 256
CENTER = 64.0
HALF = 64.0

GROUP = 16
PAIRS = GROUP // 2
SPAN = 512


def split(values):
    high = values.astype(bf16)
    return high, (values - high.astype(f32)).astype(bf16)


def group_base(g, cells, ext_len):
    first = (GROUP * g * (ext_len - WINDOW)) // (cells - 1)
    return pl.multiple_of(jnp.minimum((first // 128) * 128, ext_len - SPAN), 128)


def list_one_hot(list_ref, one_hot):
    lanes = lax.broadcasted_iota(jnp.int32, (256, 128), 0)
    for j in range(list_ref.shape[0]):
        entry = jnp.broadcast_to(list_ref[j : j + 1, :] & 255, (256, 128))
        one_hot[:, 128 * j : 128 * j + 128] = jnp.where(lanes == entry, 1.0, 0.0).astype(bf16)


def pick(source, list_ref, one_hot, target):
    rows, nodes = source.shape
    blocks = nodes // 256
    parts = [split(source[:, 256 * k : 256 * k + 256]) for k in range(blocks)]
    left = jnp.concatenate([p[0] for p in parts] + [p[1] for p in parts], axis=0)
    for j in range(list_ref.shape[0] // 2):
        both = jnp.dot(left, one_hot[:, 256 * j : 256 * j + 256], preferred_element_type=f32)
        block = jnp.concatenate([list_ref[2 * j : 2 * j + 1, :], list_ref[2 * j + 1 : 2 * j + 2, :]], axis=1) >> 8
        block = jnp.broadcast_to(block, (rows, 256))
        total = jnp.zeros((rows, 256), f32)
        for k in range(blocks):
            here = both[rows * k : rows * k + rows] + both[rows * (blocks + k) : rows * (blocks + k) + rows]
            total = jnp.where(block == k, here, total)
        target[:, 256 * j : 256 * j + 256] = total


def place(source, list_ref, one_hot, target):
    rows, nodes = target.shape
    blocks = nodes // 256
    entries = source.shape[1]
    columns = []
    for j in range(entries // 128):
        values = source[:, 128 * j : 128 * j + 128]
        high = values.astype(bf16).astype(f32)
        low = values - high
        block = jnp.broadcast_to(list_ref[j : j + 1, :] >> 8, (rows, 128))
        zero = jnp.zeros_like(values)
        masks = [block == k for k in range(blocks)]
        columns.append(
            jnp.concatenate(
                [jnp.where(m, high, zero) for m in masks] + [jnp.where(m, low, zero) for m in masks], axis=0
            ).astype(bf16)
        )
    left = jnp.concatenate(columns, axis=1)
    both = lax.dot_general(left, one_hot[...], (((1,), (1,)), ((), ())), preferred_element_type=f32)
    for k in range(blocks):
        here = both[rows * k : rows * k + rows] + both[rows * (blocks + k) : rows * (blocks + k) + rows]
        target[:, 256 * k : 256 * k + 256] += here


def build_stiffness(stiffness, paired):
    high, low = split(stiffness[...])
    none = jnp.zeros_like(high)
    rows = [[high, none, low, none], [none, high, none, low], [high, none, none, none], [none, high, none, none]]
    paired[...] = jnp.concatenate([jnp.concatenate(row, axis=1) for row in rows], axis=0)


def build_cells(index_ref, one_hot, cells, ext_len):
    def step(g, carry):
        base = group_base(g, cells, ext_len)
        local = (index_ref[pl.ds(pl.multiple_of(PAIRS * g, PAIRS), PAIRS), :] - base) & 255
        lanes = lax.broadcasted_iota(jnp.int32, (256, 128), 0)
        for h in range(PAIRS):
            entry = jnp.broadcast_to(local[h : h + 1, :], (256, 128))
            one_hot[g, 128 * h : 128 * h + 128, :] = jnp.where(lanes == entry, 1.0, 0.0).astype(bf16).T
        return carry

    lax.fori_loop(0, cells // GROUP, step, 0, unroll=2)


def run_cells(first, last, unroll, extended, index_ref, scale_ref, pair_stiffness, one_hot, summed):
    rows, ext_len = extended.shape
    cells = 2 * index_ref.shape[0]
    row_tiles = rows // 8

    def step(g, carry):
        base = group_base(g, cells, ext_len)
        source = [
            [extended[8 * o : 8 * o + 8, pl.ds(base + 128 * k, 128)] for k in range(4)] for o in range(row_tiles)
        ]
        at = pl.multiple_of(PAIRS * g, PAIRS)
        local = index_ref[pl.ds(at, PAIRS), :] - base
        scales = scale_ref[pl.ds(at, PAIRS), :]
        values, upper = [], []
        for h in range(PAIRS):
            position = jnp.broadcast_to(local[h : h + 1, :], (8, 128))
            block, lane = position >> 7, position & 127
            tiles = []
            for o in range(row_tiles):
                tile = jnp.take_along_axis(source[o][0], lane, axis=1)
                for k in range(1, 4):
                    tile = jnp.where(block == k, jnp.take_along_axis(source[o][k], lane, axis=1), tile)
                tiles.append(tile)
            values.append(jnp.concatenate(split(jnp.concatenate(tiles, axis=0)), axis=1))
            upper.append(jnp.concatenate([block] * row_tiles, axis=0) >= 2)
        images = jnp.dot(jnp.concatenate(values, axis=0), pair_stiffness[...], preferred_element_type=f32)
        images = images[:, :128] + images[:, 128:]
        columns = []
        for h in range(PAIRS):
            image = images[rows * h : rows * h + rows] * jnp.broadcast_to(scales[h : h + 1, :], (rows, 128))
            high = image.astype(bf16).astype(f32)
            low = image - high
            zero = jnp.zeros_like(image)
            columns.append(
                jnp.concatenate(
                    [
                        jnp.where(upper[h], zero, high),
                        jnp.where(upper[h], high, zero),
                        jnp.where(upper[h], zero, low),
                        jnp.where(upper[h], low, zero),
                    ],
                    axis=0,
                ).astype(bf16)
            )
        left = jnp.concatenate(columns, axis=1)
        both = jnp.dot(left, one_hot[g], preferred_element_type=f32)
        added = both[: 2 * rows] + both[2 * rows :]
        summed[:, pl.ds(base, 256)] += added[:rows]
        summed[:, pl.ds(base + 256, 256)] += added[rows:]
        return carry

    lax.fori_loop(first, last, step, 0, unroll=unroll)


def kernel(
    n_domain,
    orbitals,
    others,
    potential,
    index_ref,
    scale_ref,
    up_list,
    down_list,
    stiffness,
    rotation,
    out,
    pair_stiffness,
    one_hot,
    up_hot,
    down_hot,
    extended,
    sums,
    up_out,
    down_out,
    up_back,
    down_back,
    current,
    panel,
    others_sems,
    ghost_send,
    ghost_recv,
    back_send,
    back_recv,
    filt_sems,
):
    rows, nodes = orbitals.shape
    rim = up_out.shape[2]
    ext_len = extended.shape[2]
    cells = 2 * index_ref.shape[0]
    groups = cells // GROUP
    low_end = 288 // GROUP
    high_start = groups - low_end
    rest = others.shape[0]
    half = out.shape[0]

    me = lax.axis_index("domain")
    band = lax.axis_index("band")
    above, below = lax.rem(me + 1, n_domain), lax.rem(me + n_domain - 1, n_domain)
    mate = 1 - band

    barrier = pltpu.get_barrier_semaphore()
    for target in ({"domain": above}, {"domain": below}, {"band": mate}):
        pl.semaphore_signal(barrier, inc=1, device_id=target, device_id_type=MESH)

    other_rows = pl.ds(pl.multiple_of(2 * rows + rest * band, 8), rest)
    own_others = pltpu.make_async_copy(others, panel.at[other_rows, :], others_sems.at[0])
    own_others.start()
    build_stiffness(stiffness, pair_stiffness)
    list_one_hot(up_list, up_hot)
    list_one_hot(down_list, down_hot)

    def send_ghosts(source, step):
        pick(source, up_list, up_hot, up_out.at[step])
        up = pltpu.make_async_remote_copy(
            src_ref=up_out.at[step],
            dst_ref=extended.at[step, :, pl.ds(0, rim)],
            send_sem=ghost_send.at[step, 0],
            recv_sem=ghost_recv.at[step, 0],
            device_id={"domain": above},
            device_id_type=MESH,
        )
        if step == 0:
            pl.semaphore_wait(barrier, 3)
        up.start()
        pick(source, down_list, down_hot, down_out.at[step])
        down = pltpu.make_async_remote_copy(
            src_ref=down_out.at[step],
            dst_ref=extended.at[step, :, pl.ds(rim + nodes, rim)],
            send_sem=ghost_send.at[step, 1],
            recv_sem=ghost_recv.at[step, 1],
            device_id={"domain": below},
            device_id_type=MESH,
        )
        down.start()
        extended[step, :, rim : rim + nodes] = source[...]
        sums[step] = jnp.zeros((rows, ext_len), f32)
        return up, down

    def send_back(step, lower):
        copy = pltpu.make_async_remote_copy(
            src_ref=sums.at[step, :, pl.ds(0 if lower else rim + nodes, rim)],
            dst_ref=(up_back if lower else down_back).at[step],
            send_sem=back_send.at[step, 0 if lower else 1],
            recv_sem=back_recv.at[step, 0 if lower else 1],
            device_id={"domain": below if lower else above},
            device_id_type=MESH,
        )
        copy.start()
        return copy

    def cells_from(step, first, last, unroll):
        run_cells(
            first,
            last,
            unroll,
            extended.at[step],
            index_ref,
            scale_ref,
            pair_stiffness,
            one_hot,
            sums.at[step],
        )

    def operate(step, ghosts):
        up, down = ghosts
        up.wait()
        cells_from(step, 0, low_end, 6)
        lower = send_back(step, True)
        down.wait()
        cells_from(step, high_start, groups, 6)
        upper = send_back(step, False)
        cells_from(step, low_end, high_start, 6)
        return lower, upper

    def collect(step, backs, target):
        lower, upper = backs
        target[...] = sums[step, :, rim : rim + nodes]
        lower.wait()
        place(up_back.at[step], up_list, up_hot, target)
        upper.wait()
        place(down_back.at[step], down_list, down_hot, target)

    ghosts = send_ghosts(orbitals, 0)
    mate_others = pltpu.make_async_remote_copy(
        src_ref=others,
        dst_ref=panel.at[other_rows, :],
        send_sem=others_sems.at[1],
        recv_sem=others_sems.at[2],
        device_id={"band": mate},
        device_id_type=MESH,
    )
    mate_others.start()
    build_cells(index_ref, one_hot, cells, ext_len)
    backs = operate(0, ghosts)
    collect(0, backs, current)
    current[...] = (current[...] + potential[...] * orbitals[...] - CENTER * orbitals[...]) * (1.0 / HALF)
    ghosts = send_ghosts(current, 1)
    backs = operate(1, ghosts)

    mine = pl.ds(pl.multiple_of(rows * band, 8), rows)
    collect(1, backs, panel.at[mine, :])
    for k in range(nodes // 256):
        cut = slice(256 * k, 256 * k + 256)
        now = current[:, cut]
        panel[mine, cut] = (
            panel[mine, cut] + potential[:, cut] * now - CENTER * now
        ) * (2.0 / HALF) - orbitals[:, cut]
    mate_filt = pltpu.make_async_remote_copy(
        src_ref=panel.at[mine, :],
        dst_ref=panel.at[mine, :],
        send_sem=filt_sems.at[0],
        recv_sem=filt_sems.at[1],
        device_id={"band": mate},
        device_id_type=MESH,
    )
    mate_filt.start()
    own_others.wait()
    mate_others.wait()
    mate_filt.wait()
    weights = rotation[:, pl.ds(pl.multiple_of(band * half, 128), half)].T
    left = jnp.concatenate(split(weights), axis=0)
    for k in range(nodes // 256):
        cut = slice(256 * k, 256 * k + 256)
        high, low = split(panel[:, cut])
        main = jnp.dot(left, high, preferred_element_type=f32)
        out[:, cut] = main[:half] + main[half:] + jnp.dot(left[:half], low, preferred_element_type=f32)


def body(
    orbitals, others, potential, cell_scale, connectivity, send_up, send_down, stiffness, rotation
):
    rows, nodes = orbitals.shape
    rest = others.shape[0]
    rim = send_up.shape[0]
    npc, cells = connectivity.shape
    ext_len = nodes + 2 * rim
    panel = rotation.shape[0]
    half = panel // lax.axis_size("band")
    index = connectivity.T.reshape(cells // 2, 2 * npc)
    scale = jnp.repeat(cell_scale, npc).reshape(cells // 2, 2 * npc)
    vmem = pl.BlockSpec(memory_space=pltpu.VMEM)
    return pl.pallas_call(
        functools.partial(kernel, lax.axis_size("domain")),
        out_shape=jax.ShapeDtypeStruct((half, nodes), f32),
        in_specs=[vmem, pl.BlockSpec(memory_space=pl.ANY)] + [vmem] * 7,
        out_specs=vmem,
        scratch_shapes=[
            pltpu.VMEM((4 * npc, 4 * npc), bf16),
            pltpu.VMEM((cells // GROUP, GROUP * npc, 256), bf16),
            pltpu.VMEM((256, rim), bf16),
            pltpu.VMEM((256, rim), bf16),
            pltpu.VMEM((2, rows, ext_len), f32),
            pltpu.VMEM((2, rows, ext_len), f32),
            pltpu.VMEM((2, rows, rim), f32),
            pltpu.VMEM((2, rows, rim), f32),
            pltpu.VMEM((2, rows, rim), f32),
            pltpu.VMEM((2, rows, rim), f32),
            pltpu.VMEM((rows, nodes), f32),
            pltpu.VMEM((panel, nodes), f32),
            pltpu.SemaphoreType.DMA((3,)),
            pltpu.SemaphoreType.DMA((2, 2)),
            pltpu.SemaphoreType.DMA((2, 2)),
            pltpu.SemaphoreType.DMA((2, 2)),
            pltpu.SemaphoreType.DMA((2, 2)),
            pltpu.SemaphoreType.DMA((2,)),
        ],
        compiler_params=pltpu.CompilerParams(
            collective_id=0, has_side_effects=True, vmem_limit_bytes=52 * 2**20
        ),
        name="filter_rotate",
    )(
        orbitals,
        others,
        potential.reshape(1, nodes),
        index,
        scale,
        send_up.reshape(rim // 128, 128),
        send_down.reshape(rim // 128, 128),
        stiffness,
        rotation,
    )


def solution(mesh):
    placed = (
        P("band", "domain"),
        P("band", "domain"),
        P("domain"),
        P("domain"),
        P(None, "domain"),
        P("domain"),
        P("domain"),
        P(),
        P(),
    )
    return jax.shard_map(
        body, mesh=mesh, in_specs=placed, out_specs=P("band", "domain"), check_vma=False
    )
```

```python
import functools

import jax
import jax.numpy as jnp
from jax import lax
from jax.experimental import pallas as pl
from jax.experimental.pallas import tpu as pltpu
from jax.sharding import PartitionSpec as P

bf16 = jnp.bfloat16
f32 = jnp.float32
MESH = pl.DeviceIdType.MESH

WINDOW = 256
CENTER = 64.0
HALF = 64.0

GROUP = 16
PAIRS = GROUP // 2
SPAN = 512


def split(values):
    high = values.astype(bf16)
    return high, (values - high.astype(f32)).astype(bf16)


def group_base(g, cells, ext_len):
    first = (GROUP * g * (ext_len - WINDOW)) // (cells - 1)
    return pl.multiple_of(jnp.minimum((first // 128) * 128, ext_len - SPAN), 128)


def list_one_hot(list_ref, one_hot):
    lanes = lax.broadcasted_iota(jnp.int32, (256, 128), 0)
    for j in range(list_ref.shape[0]):
        entry = jnp.broadcast_to(list_ref[j : j + 1, :] & 255, (256, 128))
        one_hot[:, 128 * j : 128 * j + 128] = jnp.where(lanes == entry, 1.0, 0.0).astype(bf16)


def pick(source, list_ref, one_hot, target):
    rows, nodes = source.shape
    blocks = nodes // 256
    parts = [split(source[:, 256 * k : 256 * k + 256]) for k in range(blocks)]
    left = jnp.concatenate([p[0] for p in parts] + [p[1] for p in parts], axis=0)
    for j in range(list_ref.shape[0] // 2):
        both = jnp.dot(left, one_hot[:, 256 * j : 256 * j + 256], preferred_element_type=f32)
        block = jnp.concatenate([list_ref[2 * j : 2 * j + 1, :], list_ref[2 * j + 1 : 2 * j + 2, :]], axis=1) >> 8
        block = jnp.broadcast_to(block, (rows, 256))
        total = jnp.zeros((rows, 256), f32)
        for k in range(blocks):
            here = both[rows * k : rows * k + rows] + both[rows * (blocks + k) : rows * (blocks + k) + rows]
            total = jnp.where(block == k, here, total)
        target[:, 256 * j : 256 * j + 256] = total


def place(source, list_ref, one_hot, target):
    rows, nodes = target.shape
    blocks = nodes // 256
    entries = source.shape[1]
    columns = []
    for j in range(entries // 128):
        values = source[:, 128 * j : 128 * j + 128]
        high = values.astype(bf16).astype(f32)
        low = values - high
        block = jnp.broadcast_to(list_ref[j : j + 1, :] >> 8, (rows, 128))
        zero = jnp.zeros_like(values)
        masks = [block == k for k in range(blocks)]
        columns.append(
            jnp.concatenate(
                [jnp.where(m, high, zero) for m in masks] + [jnp.where(m, low, zero) for m in masks], axis=0
            ).astype(bf16)
        )
    left = jnp.concatenate(columns, axis=1)
    both = lax.dot_general(left, one_hot[...], (((1,), (1,)), ((), ())), preferred_element_type=f32)
    for k in range(blocks):
        here = both[rows * k : rows * k + rows] + both[rows * (blocks + k) : rows * (blocks + k) + rows]
        target[:, 256 * k : 256 * k + 256] += here


def build_stiffness(stiffness, paired):
    high, low = split(stiffness[...])
    none = jnp.zeros_like(high)
    rows = [[high, none, low, none], [none, high, none, low], [high, none, none, none], [none, high, none, none]]
    paired[...] = jnp.concatenate([jnp.concatenate(row, axis=1) for row in rows], axis=0)


def build_cells(index_ref, one_hot, cells, ext_len):
    def step(g, carry):
        base = group_base(g, cells, ext_len)
        local = (index_ref[pl.ds(pl.multiple_of(PAIRS * g, PAIRS), PAIRS), :] - base) & 255
        lanes = lax.broadcasted_iota(jnp.int32, (256, 128), 0)
        for h in range(PAIRS):
            entry = jnp.broadcast_to(local[h : h + 1, :], (256, 128))
            one_hot[g, 128 * h : 128 * h + 128, :] = jnp.where(lanes == entry, 1.0, 0.0).astype(bf16).T
        return carry

    lax.fori_loop(0, cells // GROUP, step, 0, unroll=2)


def run_cells(first, last, unroll, extended, index_ref, scale_ref, pair_stiffness, one_hot, summed):
    rows, ext_len = extended.shape
    cells = 2 * index_ref.shape[0]
    row_tiles = rows // 8

    def step(g, carry):
        base = group_base(g, cells, ext_len)
        source = [
            [extended[8 * o : 8 * o + 8, pl.ds(base + 128 * k, 128)] for k in range(4)] for o in range(row_tiles)
        ]
        at = pl.multiple_of(PAIRS * g, PAIRS)
        local = index_ref[pl.ds(at, PAIRS), :] - base
        scales = scale_ref[pl.ds(at, PAIRS), :]
        values, upper = [], []
        for h in range(PAIRS):
            position = jnp.broadcast_to(local[h : h + 1, :], (8, 128))
            block, lane = position >> 7, position & 127
            tiles = []
            for o in range(row_tiles):
                tile = jnp.take_along_axis(source[o][0], lane, axis=1)
                for k in range(1, 4):
                    tile = jnp.where(block == k, jnp.take_along_axis(source[o][k], lane, axis=1), tile)
                tiles.append(tile)
            values.append(jnp.concatenate(split(jnp.concatenate(tiles, axis=0)), axis=1))
            upper.append(jnp.concatenate([block] * row_tiles, axis=0) >= 2)
        images = jnp.dot(jnp.concatenate(values, axis=0), pair_stiffness[...], preferred_element_type=f32)
        images = images[:, :128] + images[:, 128:]
        columns = []
        for h in range(PAIRS):
            image = images[rows * h : rows * h + rows] * jnp.broadcast_to(scales[h : h + 1, :], (rows, 128))
            high = image.astype(bf16).astype(f32)
            low = image - high
            zero = jnp.zeros_like(image)
            columns.append(
                jnp.concatenate(
                    [
                        jnp.where(upper[h], zero, high),
                        jnp.where(upper[h], high, zero),
                        jnp.where(upper[h], zero, low),
                        jnp.where(upper[h], low, zero),
                    ],
                    axis=0,
                ).astype(bf16)
            )
        left = jnp.concatenate(columns, axis=1)
        both = jnp.dot(left, one_hot[g], preferred_element_type=f32)
        added = both[: 2 * rows] + both[2 * rows :]
        summed[:, pl.ds(base, 256)] += added[:rows]
        summed[:, pl.ds(base + 256, 256)] += added[rows:]
        return carry

    lax.fori_loop(first, last, step, 0, unroll=unroll)


def pair_rows(block, turn, target):
    turn[...] = jnp.concatenate([block, pltpu.roll(block, 127, 1)], axis=0).T
    target[...] = turn[pl.ds(0, 64, stride=2), :]


def pieces(weights):
    high, low = split(weights)
    return jnp.concatenate([high, high, low], axis=1)


def times(weights, values):
    high, low = split(values)
    return jnp.dot(weights, jnp.concatenate([high, low, high], axis=0), preferred_element_type=f32)


def kernel(
    n_domain,
    orbitals,
    others,
    potential,
    connectivity,
    cell_scale,
    up_list,
    down_list,
    stiffness,
    rotation,
    out,
    pair_stiffness,
    one_hot,
    up_hot,
    down_hot,
    index_ref,
    scale_ref,
    index_turn,
    scale_turn,
    extended,
    sums,
    up_out,
    down_out,
    up_back,
    down_back,
    current,
    own_others,
    mate_others,
    own_filt,
    mate_filt,
    rotated,
    own_sem,
    others_send,
    others_recv,
    ghost_send,
    ghost_recv,
    back_send,
    back_recv,
    filt_send,
    filt_recv,
    out_sems,
):
    rows, nodes = orbitals.shape
    rim = up_out.shape[2]
    ext_len = extended.shape[2]
    cells = connectivity.shape[1]
    groups = cells // GROUP
    low_end = 288 // GROUP
    high_start = groups - low_end
    rest = others.shape[0]
    half = out.shape[0]
    piece = nodes // filt_send.shape[0]

    me = lax.axis_index("domain")
    band = lax.axis_index("band")
    above, below = lax.rem(me + 1, n_domain), lax.rem(me + n_domain - 1, n_domain)
    mate = 1 - band

    barrier = pltpu.get_barrier_semaphore()
    for target in ({"domain": above}, {"domain": below}, {"band": mate}):
        pl.semaphore_signal(barrier, inc=1, device_id=target, device_id_type=MESH)

    own_copy = pltpu.make_async_copy(others, own_others, own_sem)
    own_copy.start()
    list_one_hot(up_list, up_hot)
    list_one_hot(down_list, down_hot)

    def send_ghosts(source, step):
        pick(source, up_list, up_hot, up_out.at[step])
        up = pltpu.make_async_remote_copy(
            src_ref=up_out.at[step],
            dst_ref=extended.at[step, :, pl.ds(0, rim)],
            send_sem=ghost_send.at[step, 0],
            recv_sem=ghost_recv.at[step, 0],
            device_id={"domain": above},
            device_id_type=MESH,
        )
        if step == 0:
            pl.semaphore_wait(barrier, 3)
        up.start()
        pick(source, down_list, down_hot, down_out.at[step])
        down = pltpu.make_async_remote_copy(
            src_ref=down_out.at[step],
            dst_ref=extended.at[step, :, pl.ds(rim + nodes, rim)],
            send_sem=ghost_send.at[step, 1],
            recv_sem=ghost_recv.at[step, 1],
            device_id={"domain": below},
            device_id_type=MESH,
        )
        down.start()
        extended[step, :, rim : rim + nodes] = source[...]
        sums[step] = jnp.zeros((rows, ext_len), f32)
        return up, down

    def send_back(step, lower):
        copy = pltpu.make_async_remote_copy(
            src_ref=sums.at[step, :, pl.ds(0 if lower else rim + nodes, rim)],
            dst_ref=(up_back if lower else down_back).at[step],
            send_sem=back_send.at[step, 0 if lower else 1],
            recv_sem=back_recv.at[step, 0 if lower else 1],
            device_id={"domain": below if lower else above},
            device_id_type=MESH,
        )
        copy.start()
        return copy

    def send_others(step):
        cut = pl.ds(0, rest // 3 * 2) if step == 0 else pl.ds(rest // 3 * 2, rest // 3)
        copy = pltpu.make_async_remote_copy(
            src_ref=own_others.at[cut, :],
            dst_ref=mate_others.at[cut, :],
            send_sem=others_send.at[step],
            recv_sem=others_recv.at[step],
            device_id={"band": mate},
            device_id_type=MESH,
        )
        copy.start()
        return copy

    def cells_from(step, first, last, unroll):
        run_cells(
            first,
            last,
            unroll,
            extended.at[step],
            index_ref,
            scale_ref,
            pair_stiffness,
            one_hot,
            sums.at[step],
        )

    up, down = send_ghosts(orbitals, 0)
    build_stiffness(stiffness, pair_stiffness)
    for k in range(cells // 128):
        cut = slice(128 * k, 128 * k + 128)
        pair_rows(connectivity[:, cut], index_turn, index_ref.at[64 * k : 64 * k + 64, :])
        pair_rows(
            jnp.broadcast_to(cell_scale[k : k + 1, :], (64, 128)), scale_turn, scale_ref.at[64 * k : 64 * k + 64, :]
        )
    build_cells(index_ref, one_hot, cells, ext_len)
    own_copy.wait()
    up.wait()
    others_0 = send_others(0)
    cells_from(0, 0, low_end, 9)
    lower = send_back(0, True)
    down.wait()
    cells_from(0, high_start, groups, 9)
    upper = send_back(0, False)
    cells_from(0, low_end, high_start, 6)
    current[...] = sums[0, :, rim : rim + nodes]
    lower.wait()
    place(up_back.at[0], up_list, up_hot, current)
    upper.wait()
    place(down_back.at[0], down_list, down_hot, current)
    for k in range(nodes // 256):
        cut = slice(256 * k, 256 * k + 256)
        before = orbitals[:, cut]
        current[:, cut] = (current[:, cut] + potential[:, cut] * before - CENTER * before) * (1.0 / HALF)

    up, down = send_ghosts(current, 1)
    cells_from(1, low_end, high_start, 6)
    up.wait()
    others_1 = send_others(1)
    cells_from(1, 0, low_end, 9)
    lower = send_back(1, True)
    down.wait()
    cells_from(1, high_start, groups, 9)
    upper = send_back(1, False)
    own_filt[...] = sums[1, :, rim : rim + nodes]

    columns = pl.ds(pl.multiple_of(band * half, 128), half)

    def weights_of(first, count):
        return rotation[pl.ds(pl.multiple_of(first, 8), count), columns].T

    others_0.wait()
    others_1.wait()
    high, low = split(
        jnp.concatenate([weights_of(2 * rows + rest * band, rest), weights_of(2 * rows + rest * mate, rest)], axis=1)
    )
    both_parts = jnp.concatenate([high, low], axis=0)

    def other_products(k, carry):
        cut = pl.ds(pl.multiple_of(256 * k, 256), 256)
        high_values, low_values = split(jnp.concatenate([own_others[:, cut], mate_others[:, cut]], axis=0))
        main = jnp.dot(both_parts, high_values, preferred_element_type=f32)
        rotated[:, cut] = main[:half] + main[half:] + jnp.dot(high, low_values, preferred_element_type=f32)
        return carry

    lax.fori_loop(0, nodes // 256, other_products, 0, unroll=2)
    own_weights = pieces(weights_of(rows * band, rows))
    mate_weights = pieces(weights_of(rows * mate, rows))

    lower.wait()
    place(up_back.at[1], up_list, up_hot, own_filt)
    upper.wait()
    place(down_back.at[1], down_list, down_hot, own_filt)
    copies = []
    for k in range(nodes // piece):
        cut = slice(piece * k, piece * k + piece)
        now = current[:, cut]
        own_filt[:, cut] = (own_filt[:, cut] + potential[:, cut] * now - CENTER * now) * (2.0 / HALF) - orbitals[:, cut]
        copy = pltpu.make_async_remote_copy(
            src_ref=own_filt.at[:, pl.ds(piece * k, piece)],
            dst_ref=mate_filt.at[:, pl.ds(piece * k, piece)],
            send_sem=filt_send.at[k],
            recv_sem=filt_recv.at[k],
            device_id={"band": mate},
            device_id_type=MESH,
        )
        copy.start()
        copies.append(copy)
    for k in range(nodes // 256):
        cut = slice(256 * k, 256 * k + 256)
        rotated[:, cut] += times(own_weights, own_filt[:, cut])
    writes = []
    for k in range(nodes // piece):
        copies[k].wait()
        for j in range(piece // 256):
            cut = slice(piece * k + 256 * j, piece * k + 256 * j + 256)
            rotated[:, cut] += times(mate_weights, mate_filt[:, cut])
        write = pltpu.make_async_copy(
            rotated.at[:, pl.ds(piece * k, piece)], out.at[:, pl.ds(piece * k, piece)], out_sems.at[k]
        )
        write.start()
        writes.append(write)
    for write in writes:
        write.wait()


def body(
    orbitals, others, potential, cell_scale, connectivity, send_up, send_down, stiffness, rotation
):
    rows, nodes = orbitals.shape
    rest = others.shape[0]
    rim = send_up.shape[0]
    npc, cells = connectivity.shape
    ext_len = nodes + 2 * rim
    panel = rotation.shape[0]
    half = panel // lax.axis_size("band")
    parts = 4
    vmem = pl.BlockSpec(memory_space=pltpu.VMEM)
    hbm = pl.BlockSpec(memory_space=pl.ANY)
    return pl.pallas_call(
        functools.partial(kernel, lax.axis_size("domain")),
        out_shape=jax.ShapeDtypeStruct((half, nodes), f32),
        in_specs=[vmem, hbm] + [vmem] * 7,
        out_specs=hbm,
        scratch_shapes=[
            pltpu.VMEM((4 * npc, 4 * npc), bf16),
            pltpu.VMEM((cells // GROUP, GROUP * npc, 256), bf16),
            pltpu.VMEM((256, rim), bf16),
            pltpu.VMEM((256, rim), bf16),
            pltpu.VMEM((cells // 2, 2 * npc), jnp.int32),
            pltpu.VMEM((cells // 2, 2 * npc), f32),
            pltpu.VMEM((128, 128), jnp.int32),
            pltpu.VMEM((128, 128), f32),
            pltpu.VMEM((2, rows, ext_len), f32),
            pltpu.VMEM((2, rows, ext_len), f32),
            pltpu.VMEM((2, rows, rim), f32),
            pltpu.VMEM((2, rows, rim), f32),
            pltpu.VMEM((2, rows, rim), f32),
            pltpu.VMEM((2, rows, rim), f32),
            pltpu.VMEM((rows, nodes), f32),
            pltpu.VMEM((rest, nodes), f32),
            pltpu.VMEM((rest, nodes), f32),
            pltpu.VMEM((rows, nodes), f32),
            pltpu.VMEM((rows, nodes), f32),
            pltpu.VMEM((half, nodes), f32),
            pltpu.SemaphoreType.DMA,
            pltpu.SemaphoreType.DMA((2,)),
            pltpu.SemaphoreType.DMA((2,)),
            pltpu.SemaphoreType.DMA((2, 2)),
            pltpu.SemaphoreType.DMA((2, 2)),
            pltpu.SemaphoreType.DMA((2, 2)),
            pltpu.SemaphoreType.DMA((2, 2)),
            pltpu.SemaphoreType.DMA((parts,)),
            pltpu.SemaphoreType.DMA((parts,)),
            pltpu.SemaphoreType.DMA((parts,)),
        ],
        compiler_params=pltpu.CompilerParams(
            collective_id=0, has_side_effects=True, vmem_limit_bytes=52 * 2**20
        ),
        name="filter_rotate",
    )(
        orbitals,
        others,
        potential.reshape(1, nodes),
        connectivity,
        cell_scale.reshape(cells // 128, 128),
        send_up.reshape(rim // 128, 128),
        send_down.reshape(rim // 128, 128),
        stiffness,
        rotation,
    )


def solution(mesh):
    placed = (
        P("band", "domain"),
        P("band", "domain"),
        P("domain"),
        P("domain"),
        P(None, "domain"),
        P("domain"),
        P("domain"),
        P(),
        P(),
    )
    return jax.shard_map(
        body, mesh=mesh, in_specs=placed, out_specs=P("band", "domain"), check_vma=False
    )
```

```python
import functools

import jax
import jax.numpy as jnp
from jax import lax
from jax.experimental import pallas as pl
from jax.experimental.pallas import tpu as pltpu
from jax.sharding import PartitionSpec as P

bf16 = jnp.bfloat16
f32 = jnp.float32
MESH = pl.DeviceIdType.MESH

WINDOW = 256
CENTER = 64.0
HALF = 64.0

GROUP = 16
PAIRS = GROUP // 2
SPAN = 512


def split(values):
    high = values.astype(bf16)
    return high, (values - high.astype(f32)).astype(bf16)


def group_base(g, cells, ext_len):
    first = (GROUP * g * (ext_len - WINDOW)) // (cells - 1)
    return pl.multiple_of(jnp.minimum((first // 128) * 128, ext_len - SPAN), 128)


def list_one_hot(list_ref, one_hot):
    lanes = lax.broadcasted_iota(jnp.int32, (256, 128), 0)
    for j in range(list_ref.shape[0]):
        entry = jnp.broadcast_to(list_ref[j : j + 1, :] & 255, (256, 128))
        one_hot[:, 128 * j : 128 * j + 128] = jnp.where(lanes == entry, 1.0, 0.0).astype(bf16)


def pick(source, list_ref, one_hot, target):
    rows, nodes = source.shape
    blocks = nodes // 256
    parts = [split(source[:, 256 * k : 256 * k + 256]) for k in range(blocks)]
    left = jnp.concatenate([p[0] for p in parts] + [p[1] for p in parts], axis=0)
    for j in range(list_ref.shape[0] // 2):
        both = jnp.dot(left, one_hot[:, 256 * j : 256 * j + 256], preferred_element_type=f32)
        block = jnp.concatenate([list_ref[2 * j : 2 * j + 1, :], list_ref[2 * j + 1 : 2 * j + 2, :]], axis=1) >> 8
        block = jnp.broadcast_to(block, (rows, 256))
        total = jnp.zeros((rows, 256), f32)
        for k in range(blocks):
            here = both[rows * k : rows * k + rows] + both[rows * (blocks + k) : rows * (blocks + k) + rows]
            total = jnp.where(block == k, here, total)
        target[:, 256 * j : 256 * j + 256] = total


def place(source, list_ref, one_hot, target):
    rows, nodes = target.shape
    blocks = nodes // 256
    entries = source.shape[1]
    columns = []
    for j in range(entries // 128):
        high, low = split(source[:, 128 * j : 128 * j + 128])
        block = (list_ref[j : j + 1, :] >> 8).astype(f32).astype(bf16)
        block = jnp.broadcast_to(block, (rows, 128))
        zero = jnp.zeros_like(high)
        masks = [block == k for k in range(blocks)]
        columns.append(
            jnp.concatenate(
                [jnp.where(m, high, zero) for m in masks] + [jnp.where(m, low, zero) for m in masks], axis=0
            )
        )
    left = jnp.concatenate(columns, axis=1)
    both = lax.dot_general(left, one_hot[...], (((1,), (1,)), ((), ())), preferred_element_type=f32)
    for k in range(blocks):
        here = both[rows * k : rows * k + rows] + both[rows * (blocks + k) : rows * (blocks + k) + rows]
        target[:, 256 * k : 256 * k + 256] += here


def build_stiffness(stiffness, paired):
    high, low = split(stiffness[...])
    none = jnp.zeros_like(high)
    rows = [[high, none, low, none], [none, high, none, low], [high, none, none, none], [none, high, none, none]]
    paired[...] = jnp.concatenate([jnp.concatenate(row, axis=1) for row in rows], axis=0)


def build_cells(index_ref, one_hot, cells, ext_len):
    def step(g, carry):
        base = group_base(g, cells, ext_len)
        local = (index_ref[pl.ds(pl.multiple_of(PAIRS * g, PAIRS), PAIRS), :] - base) & 255
        local = local.astype(f32).astype(bf16)
        lanes = lax.broadcasted_iota(jnp.int32, (128, 256), 1).astype(f32).astype(bf16)
        one, zero = jnp.ones((128, 256), bf16), jnp.zeros((128, 256), bf16)
        for h in range(PAIRS):
            entry = jnp.broadcast_to(local[h : h + 1, :], (128, 128)).T
            entry = jnp.concatenate([entry, entry], axis=1)
            one_hot[g, 128 * h : 128 * h + 128, :] = jnp.where(lanes == entry, one, zero)
        return carry

    lax.fori_loop(0, cells // GROUP, step, 0, unroll=4)


def run_cells(first, count, sign, unroll, extended, index_ref, scale_ref, pair_stiffness, one_hot, summed):
    rows, ext_len = extended.shape
    cells = 2 * index_ref.shape[0]
    row_tiles = rows // 8

    def step(i, carry):
        g = first + sign * i
        base = group_base(g, cells, ext_len)
        source = [
            [extended[8 * o : 8 * o + 8, pl.ds(base + 128 * k, 128)] for k in range(4)] for o in range(row_tiles)
        ]
        at = pl.multiple_of(PAIRS * g, PAIRS)
        local = index_ref[pl.ds(at, PAIRS), :] - base
        scales = scale_ref[pl.ds(at, PAIRS), :]
        values, upper = [], []
        for h in range(PAIRS):
            position = jnp.broadcast_to(local[h : h + 1, :], (8, 128))
            block, lane = position >> 7, position & 127
            tiles = []
            for o in range(row_tiles):
                tile = jnp.take_along_axis(source[o][0], lane, axis=1)
                for k in range(1, 4):
                    tile = jnp.where(block == k, jnp.take_along_axis(source[o][k], lane, axis=1), tile)
                tiles.append(tile)
            values.append(jnp.concatenate(split(jnp.concatenate(tiles, axis=0)), axis=1))
            upper.append(jnp.concatenate([block] * row_tiles, axis=0) >= 2)
        images = jnp.dot(jnp.concatenate(values, axis=0), pair_stiffness[...], preferred_element_type=f32)
        images = images[:, :128] + images[:, 128:]
        columns = []
        for h in range(PAIRS):
            image = images[rows * h : rows * h + rows] * jnp.broadcast_to(scales[h : h + 1, :], (rows, 128))
            high = image.astype(bf16).astype(f32)
            low = image - high
            zero = jnp.zeros_like(image)
            columns.append(
                jnp.concatenate(
                    [
                        jnp.where(upper[h], zero, high),
                        jnp.where(upper[h], high, zero),
                        jnp.where(upper[h], zero, low),
                        jnp.where(upper[h], low, zero),
                    ],
                    axis=0,
                ).astype(bf16)
            )
        left = jnp.concatenate(columns, axis=1)
        both = jnp.dot(left, one_hot[g], preferred_element_type=f32)
        added = both[: 2 * rows] + both[2 * rows :]
        summed[:, pl.ds(base, 256)] += added[:rows]
        summed[:, pl.ds(base + 256, 256)] += added[rows:]
        return carry

    lax.fori_loop(0, count, step, 0, unroll=unroll)


def pair_rows(block, turn, target):
    turn[...] = jnp.concatenate([block, pltpu.roll(block, 127, 1)], axis=0).T
    target[...] = turn[pl.ds(0, 64, stride=2), :]


def pieces(weights):
    high, low = split(weights)
    return jnp.concatenate([high, high, low], axis=1)


def times(weights, values):
    high, low = split(values)
    return jnp.dot(weights, jnp.concatenate([high, low, high], axis=0), preferred_element_type=f32)


def kernel(
    n_domain,
    hbm_orbitals,
    others,
    hbm_potential,
    hbm_connectivity,
    hbm_cell_scale,
    hbm_up_list,
    hbm_down_list,
    hbm_stiffness,
    hbm_rotation,
    out,
    orbitals,
    potential,
    connectivity,
    cell_scale,
    up_list,
    down_list,
    stiffness,
    rotation,
    pair_stiffness,
    one_hot,
    up_hot,
    down_hot,
    index_ref,
    scale_ref,
    index_turn,
    scale_turn,
    extended,
    sums,
    up_out,
    down_out,
    up_back,
    down_back,
    current,
    own_others,
    mate_others,
    own_filt,
    mate_filt,
    rotated,
    own_sem,
    others_send,
    others_recv,
    ghost_send,
    ghost_recv,
    back_send,
    back_recv,
    filt_send,
    filt_recv,
    out_sems,
    in_sems,
):
    rows, nodes = orbitals.shape
    rim = up_out.shape[2]
    ext_len = extended.shape[2]
    cells = connectivity.shape[1]
    groups = cells // GROUP
    low_end = 288 // GROUP
    high_start = groups - low_end
    low_half, high_half = low_end // 2, groups - low_end // 2
    low_cut = GROUP * low_half * (ext_len - WINDOW) // (cells - 1) // 128 * 128
    high_cut = GROUP * (high_half - 1) * (ext_len - WINDOW) // (cells - 1) // 128 * 128 + SPAN
    rest = others.shape[0]
    half = out.shape[0]
    piece = nodes // filt_send.shape[0]

    me = lax.axis_index("domain")
    band = lax.axis_index("band")
    above, below = lax.rem(me + 1, n_domain), lax.rem(me + n_domain - 1, n_domain)
    mate = 1 - band

    barrier = pltpu.get_barrier_semaphore()
    for target in ({"domain": above}, {"domain": below}, {"band": mate}):
        pl.semaphore_signal(barrier, inc=1, device_id=target, device_id_type=MESH)

    loads = []
    for k, (source, target) in enumerate(
        (
            (hbm_up_list, up_list),
            (hbm_orbitals, orbitals),
            (hbm_down_list, down_list),
            (hbm_connectivity, connectivity),
            (hbm_cell_scale, cell_scale),
            (hbm_stiffness, stiffness),
            (hbm_potential, potential),
            (hbm_rotation, rotation),
        )
    ):
        loads.append(pltpu.make_async_copy(source, target, in_sems.at[k]))
        loads[k].start()
    own_copy = pltpu.make_async_copy(others, own_others, own_sem)
    own_copy.start()
    loads[0].wait()
    list_one_hot(up_list, up_hot)
    loads[1].wait()
    loads[2].wait()
    list_one_hot(down_list, down_hot)

    def send_ghosts(source, step):
        pick(source, up_list, up_hot, up_out.at[step])
        up = pltpu.make_async_remote_copy(
            src_ref=up_out.at[step],
            dst_ref=extended.at[step, :, pl.ds(0, rim)],
            send_sem=ghost_send.at[step, 0],
            recv_sem=ghost_recv.at[step, 0],
            device_id={"domain": above},
            device_id_type=MESH,
        )
        if step == 0:
            pl.semaphore_wait(barrier, 3)
        up.start()
        pick(source, down_list, down_hot, down_out.at[step])
        down = pltpu.make_async_remote_copy(
            src_ref=down_out.at[step],
            dst_ref=extended.at[step, :, pl.ds(rim + nodes, rim)],
            send_sem=ghost_send.at[step, 1],
            recv_sem=ghost_recv.at[step, 1],
            device_id={"domain": below},
            device_id_type=MESH,
        )
        down.start()
        extended[step, :, rim : rim + nodes] = source[...]
        sums[step] = jnp.zeros((rows, ext_len), f32)
        return up, down

    def send_back(step, lower, part):
        edge = low_cut if lower else high_cut - rim - nodes
        first = 0 if (part == 0) == lower else edge
        count = edge if (part == 0) == lower else rim - edge
        sem = part if lower else 2 + part
        copy = pltpu.make_async_remote_copy(
            src_ref=sums.at[step, :, pl.ds(first if lower else rim + nodes + first, count)],
            dst_ref=(up_back if lower else down_back).at[step, :, pl.ds(first, count)],
            send_sem=back_send.at[step, sem],
            recv_sem=back_recv.at[step, sem],
            device_id={"domain": below if lower else above},
            device_id_type=MESH,
        )
        copy.start()
        return copy

    def lower_cells(step):
        cells_from(step, 0, low_half, 1, 9)
        first = send_back(step, True, 0)
        cells_from(step, low_half, low_end - low_half, 1, 9)
        return first, send_back(step, True, 1)

    def upper_cells(step):
        cells_from(step, groups - 1, groups - high_half, -1, 9)
        first = send_back(step, False, 0)
        cells_from(step, high_half - 1, high_half - high_start, -1, 9)
        return first, send_back(step, False, 1)

    def send_others(step):
        cut = pl.ds(0, rest // 3 * 2) if step == 0 else pl.ds(rest // 3 * 2, rest // 3)
        copy = pltpu.make_async_remote_copy(
            src_ref=own_others.at[cut, :],
            dst_ref=mate_others.at[cut, :],
            send_sem=others_send.at[step],
            recv_sem=others_recv.at[step],
            device_id={"band": mate},
            device_id_type=MESH,
        )
        copy.start()
        return copy

    def cells_from(step, first, count, sign, unroll):
        run_cells(
            first,
            count,
            sign,
            unroll,
            extended.at[step],
            index_ref,
            scale_ref,
            pair_stiffness,
            one_hot,
            sums.at[step],
        )

    up, down = send_ghosts(orbitals, 0)
    for load in loads[3:]:
        load.wait()
    build_stiffness(stiffness, pair_stiffness)
    for k in range(cells // 128):
        cut = slice(128 * k, 128 * k + 128)
        pair_rows(connectivity[:, cut], index_turn, index_ref.at[64 * k : 64 * k + 64, :])
        pair_rows(
            jnp.broadcast_to(cell_scale[k : k + 1, :], (64, 128)), scale_turn, scale_ref.at[64 * k : 64 * k + 64, :]
        )
    build_cells(index_ref, one_hot, cells, ext_len)
    own_copy.wait()
    up.wait()
    down.wait()
    others_0 = send_others(0)
    lower = lower_cells(0)
    upper = upper_cells(0)
    cells_from(0, low_end, high_start - low_end, 1, 6)
    current[...] = sums[0, :, rim : rim + nodes]
    for copy in lower:
        copy.wait()
    place(up_back.at[0], up_list, up_hot, current)
    for copy in upper:
        copy.wait()
    place(down_back.at[0], down_list, down_hot, current)
    for k in range(nodes // 256):
        cut = slice(256 * k, 256 * k + 256)
        before = orbitals[:, cut]
        current[:, cut] = (current[:, cut] + potential[:, cut] * before - CENTER * before) * (1.0 / HALF)

    up, down = send_ghosts(current, 1)
    cells_from(1, low_end, high_start - low_end, 1, 6)
    up.wait()
    lower = lower_cells(1)
    down.wait()
    others_1 = send_others(1)
    upper = upper_cells(1)
    own_filt[...] = sums[1, :, rim : rim + nodes]

    columns = pl.ds(pl.multiple_of(band * half, 128), half)

    def weights_of(first, count):
        return rotation[pl.ds(pl.multiple_of(first, 8), count), columns].T

    others_0.wait()
    others_1.wait()
    high, low = split(
        jnp.concatenate([weights_of(2 * rows + rest * band, rest), weights_of(2 * rows + rest * mate, rest)], axis=1)
    )
    both_parts = jnp.concatenate([high, low], axis=0)

    def other_products(k, carry):
        cut = pl.ds(pl.multiple_of(256 * k, 256), 256)
        high_values, low_values = split(jnp.concatenate([own_others[:, cut], mate_others[:, cut]], axis=0))
        main = jnp.dot(both_parts, high_values, preferred_element_type=f32)
        rotated[:, cut] = main[:half] + main[half:] + jnp.dot(high, low_values, preferred_element_type=f32)
        return carry

    lax.fori_loop(0, nodes // 256, other_products, 0, unroll=2)
    own_weights = pieces(weights_of(rows * band, rows))
    mate_weights = pieces(weights_of(rows * mate, rows))

    for copy in lower:
        copy.wait()
    place(up_back.at[1], up_list, up_hot, own_filt)
    for copy in upper:
        copy.wait()
    place(down_back.at[1], down_list, down_hot, own_filt)
    copies = []
    for k in range(nodes // piece):
        cut = slice(piece * k, piece * k + piece)
        now = current[:, cut]
        own_filt[:, cut] = (own_filt[:, cut] + potential[:, cut] * now - CENTER * now) * (2.0 / HALF) - orbitals[:, cut]
        copy = pltpu.make_async_remote_copy(
            src_ref=own_filt.at[:, pl.ds(piece * k, piece)],
            dst_ref=mate_filt.at[:, pl.ds(piece * k, piece)],
            send_sem=filt_send.at[k],
            recv_sem=filt_recv.at[k],
            device_id={"band": mate},
            device_id_type=MESH,
        )
        copy.start()
        copies.append(copy)
    for k in range(nodes // 256):
        cut = slice(256 * k, 256 * k + 256)
        rotated[:, cut] += times(own_weights, own_filt[:, cut])
    writes = []
    for k in range(nodes // piece):
        copies[k].wait()
        for j in range(piece // 256):
            cut = slice(piece * k + 256 * j, piece * k + 256 * j + 256)
            rotated[:, cut] += times(mate_weights, mate_filt[:, cut])
        write = pltpu.make_async_copy(
            rotated.at[:, pl.ds(piece * k, piece)], out.at[:, pl.ds(piece * k, piece)], out_sems.at[k]
        )
        write.start()
        writes.append(write)
    for write in writes:
        write.wait()


def body(
    orbitals, others, potential, cell_scale, connectivity, send_up, send_down, stiffness, rotation
):
    rows, nodes = orbitals.shape
    rest = others.shape[0]
    rim = send_up.shape[0]
    npc, cells = connectivity.shape
    ext_len = nodes + 2 * rim
    panel = rotation.shape[0]
    half = panel // lax.axis_size("band")
    parts = 4
    hbm = pl.BlockSpec(memory_space=pl.ANY)
    return pl.pallas_call(
        functools.partial(kernel, lax.axis_size("domain")),
        out_shape=jax.ShapeDtypeStruct((half, nodes), f32),
        in_specs=[hbm] * 9,
        out_specs=hbm,
        scratch_shapes=[
            pltpu.VMEM((rows, nodes), f32),
            pltpu.VMEM((1, nodes), f32),
            pltpu.VMEM((npc, cells), jnp.int32),
            pltpu.VMEM((cells // 128, 128), f32),
            pltpu.VMEM((rim // 128, 128), jnp.int32),
            pltpu.VMEM((rim // 128, 128), jnp.int32),
            pltpu.VMEM((npc, npc), f32),
            pltpu.VMEM((panel, panel), f32),
            pltpu.VMEM((4 * npc, 4 * npc), bf16),
            pltpu.VMEM((cells // GROUP, GROUP * npc, 256), bf16),
            pltpu.VMEM((256, rim), bf16),
            pltpu.VMEM((256, rim), bf16),
            pltpu.VMEM((cells // 2, 2 * npc), jnp.int32),
            pltpu.VMEM((cells // 2, 2 * npc), f32),
            pltpu.VMEM((128, 128), jnp.int32),
            pltpu.VMEM((128, 128), f32),
            pltpu.VMEM((2, rows, ext_len), f32),
            pltpu.VMEM((2, rows, ext_len), f32),
            pltpu.VMEM((2, rows, rim), f32),
            pltpu.VMEM((2, rows, rim), f32),
            pltpu.VMEM((2, rows, rim), f32),
            pltpu.VMEM((2, rows, rim), f32),
            pltpu.VMEM((rows, nodes), f32),
            pltpu.VMEM((rest, nodes), f32),
            pltpu.VMEM((rest, nodes), f32),
            pltpu.VMEM((rows, nodes), f32),
            pltpu.VMEM((rows, nodes), f32),
            pltpu.VMEM((half, nodes), f32),
            pltpu.SemaphoreType.DMA,
            pltpu.SemaphoreType.DMA((2,)),
            pltpu.SemaphoreType.DMA((2,)),
            pltpu.SemaphoreType.DMA((2, 2)),
            pltpu.SemaphoreType.DMA((2, 2)),
            pltpu.SemaphoreType.DMA((2, 4)),
            pltpu.SemaphoreType.DMA((2, 4)),
            pltpu.SemaphoreType.DMA((parts,)),
            pltpu.SemaphoreType.DMA((parts,)),
            pltpu.SemaphoreType.DMA((parts,)),
            pltpu.SemaphoreType.DMA((8,)),
        ],
        compiler_params=pltpu.CompilerParams(
            collective_id=0, has_side_effects=True, vmem_limit_bytes=64 * 2**20
        ),
        name="filter_rotate",
    )(
        orbitals,
        others,
        potential.reshape(1, nodes),
        connectivity,
        cell_scale.reshape(cells // 128, 128),
        send_up.reshape(rim // 128, 128),
        send_down.reshape(rim // 128, 128),
        stiffness,
        rotation,
    )


def solution(mesh):
    placed = (
        P("band", "domain"),
        P("band", "domain"),
        P("domain"),
        P("domain"),
        P(None, "domain"),
        P("domain"),
        P("domain"),
        P(),
        P(),
    )
    return jax.shard_map(
        body, mesh=mesh, in_specs=placed, out_specs=P("band", "domain"), check_vma=False
    )
```

```python
import functools

import jax
import jax.numpy as jnp
from jax import lax
from jax.experimental import pallas as pl
from jax.experimental.pallas import tpu as pltpu
from jax.sharding import PartitionSpec as P

bf16 = jnp.bfloat16
f32 = jnp.float32
MESH = pl.DeviceIdType.MESH

WINDOW = 256
CENTER = 64.0
HALF = 64.0

GROUP = 16
PAIRS = GROUP // 2
SPAN = 512


def split(values):
    high = values.astype(bf16)
    return high, (values - high.astype(f32)).astype(bf16)


def group_base(g, cells, ext_len):
    first = (GROUP * g * (ext_len - WINDOW)) // (cells - 1)
    return pl.multiple_of(jnp.minimum((first // 128) * 128, ext_len - SPAN), 128)


def list_one_hot(list_ref, one_hot):
    lanes = lax.broadcasted_iota(jnp.int32, (256, 128), 0)
    for j in range(list_ref.shape[0]):
        entry = jnp.broadcast_to(list_ref[j : j + 1, :] & 255, (256, 128))
        one_hot[:, 128 * j : 128 * j + 128] = jnp.where(lanes == entry, 1.0, 0.0).astype(bf16)


def pick(source, list_ref, one_hot, target):
    rows, nodes = source.shape
    blocks = nodes // 256
    parts = [split(source[:, 256 * k : 256 * k + 256]) for k in range(blocks)]
    left = jnp.concatenate([p[0] for p in parts] + [p[1] for p in parts], axis=0)
    for j in range(list_ref.shape[0] // 2):
        both = jnp.dot(left, one_hot[:, 256 * j : 256 * j + 256], preferred_element_type=f32)
        block = jnp.concatenate([list_ref[2 * j : 2 * j + 1, :], list_ref[2 * j + 1 : 2 * j + 2, :]], axis=1) >> 8
        block = jnp.broadcast_to(block, (rows, 256))
        total = jnp.zeros((rows, 256), f32)
        for k in range(blocks):
            here = both[rows * k : rows * k + rows] + both[rows * (blocks + k) : rows * (blocks + k) + rows]
            total = jnp.where(block == k, here, total)
        target[:, 256 * j : 256 * j + 256] = total


def place(source, list_ref, one_hot, target):
    rows, nodes = target.shape
    blocks = nodes // 256
    entries = source.shape[1]
    columns = []
    for j in range(entries // 128):
        high, low = split(source[:, 128 * j : 128 * j + 128])
        block = (list_ref[j : j + 1, :] >> 8).astype(f32).astype(bf16)
        block = jnp.broadcast_to(block, (rows, 128))
        zero = jnp.zeros_like(high)
        masks = [block == k for k in range(blocks)]
        columns.append(
            jnp.concatenate(
                [jnp.where(m, high, zero) for m in masks] + [jnp.where(m, low, zero) for m in masks], axis=0
            )
        )
    left = jnp.concatenate(columns, axis=1)
    both = lax.dot_general(left, one_hot[...], (((1,), (1,)), ((), ())), preferred_element_type=f32)
    for k in range(blocks):
        here = both[rows * k : rows * k + rows] + both[rows * (blocks + k) : rows * (blocks + k) + rows]
        target[:, 256 * k : 256 * k + 256] += here


def build_stiffness(stiffness, paired):
    high, low = split(stiffness[...])
    none = jnp.zeros_like(high)
    rows = [[high, none, low, none], [none, high, none, low], [high, none, none, none], [none, high, none, none]]
    paired[...] = jnp.concatenate([jnp.concatenate(row, axis=1) for row in rows], axis=0)


def build_cells(index_ref, one_hot, cells, ext_len):
    def step(g, carry):
        base = group_base(g, cells, ext_len)
        local = (index_ref[pl.ds(pl.multiple_of(PAIRS * g, PAIRS), PAIRS), :] - base) & 255
        local = local.astype(f32).astype(bf16)
        lanes = lax.broadcasted_iota(jnp.int32, (128, 256), 1).astype(f32).astype(bf16)
        one, zero = jnp.ones((128, 256), bf16), jnp.zeros((128, 256), bf16)
        for h in range(PAIRS):
            entry = jnp.broadcast_to(local[h : h + 1, :], (128, 128)).T
            entry = jnp.concatenate([entry, entry], axis=1)
            one_hot[g, 128 * h : 128 * h + 128, :] = jnp.where(lanes == entry, one, zero)
        return carry

    lax.fori_loop(0, cells // GROUP, step, 0, unroll=4)


def run_cells(first, count, sign, unroll, extended, index_ref, scale_ref, pair_stiffness, one_hot, summed):
    rows, ext_len = extended.shape
    cells = 2 * index_ref.shape[0]
    row_tiles = rows // 8

    def step(i, carry):
        g = first + sign * i
        base = group_base(g, cells, ext_len)
        source = [
            [extended[8 * o : 8 * o + 8, pl.ds(base + 128 * k, 128)] for k in range(4)] for o in range(row_tiles)
        ]
        at = pl.multiple_of(PAIRS * g, PAIRS)
        local = index_ref[pl.ds(at, PAIRS), :] - base
        scales = scale_ref[pl.ds(at, PAIRS), :]
        values, upper = [], []
        for h in range(PAIRS):
            position = jnp.broadcast_to(local[h : h + 1, :], (8, 128))
            block, lane = position >> 7, position & 127
            tiles = []
            for o in range(row_tiles):
                tile = jnp.take_along_axis(source[o][0], lane, axis=1)
                for k in range(1, 4):
                    tile = jnp.where(block == k, jnp.take_along_axis(source[o][k], lane, axis=1), tile)
                tiles.append(tile)
            values.append(jnp.concatenate(split(jnp.concatenate(tiles, axis=0)), axis=1))
            upper.append(jnp.concatenate([block] * row_tiles, axis=0) >= 2)
        images = jnp.dot(jnp.concatenate(values, axis=0), pair_stiffness[...], preferred_element_type=f32)
        images = images[:, :128] + images[:, 128:]
        columns = []
        for h in range(PAIRS):
            image = images[rows * h : rows * h + rows] * jnp.broadcast_to(scales[h : h + 1, :], (rows, 128))
            high = image.astype(bf16).astype(f32)
            low = image - high
            zero = jnp.zeros_like(image)
            columns.append(
                jnp.concatenate(
                    [
                        jnp.where(upper[h], zero, high),
                        jnp.where(upper[h], high, zero),
                        jnp.where(upper[h], zero, low),
                        jnp.where(upper[h], low, zero),
                    ],
                    axis=0,
                ).astype(bf16)
            )
        left = jnp.concatenate(columns, axis=1)
        both = jnp.dot(left, one_hot[g], preferred_element_type=f32)
        added = both[: 2 * rows] + both[2 * rows :]
        summed[:, pl.ds(base, 256)] += added[:rows]
        summed[:, pl.ds(base + 256, 256)] += added[rows:]
        return carry

    lax.fori_loop(0, count, step, 0, unroll=unroll)


def pair_rows(block, turn, target):
    turn[...] = jnp.concatenate([block, pltpu.roll(block, 127, 1)], axis=0).T
    target[...] = turn[pl.ds(0, 64, stride=2), :]


def pieces(weights):
    high, low = split(weights)
    return jnp.concatenate([high, high, low], axis=1)


def times(weights, values):
    high, low = split(values)
    return jnp.dot(weights, jnp.concatenate([high, low, high], axis=0), preferred_element_type=f32)


def kernel(
    n_domain,
    hbm_orbitals,
    others,
    hbm_potential,
    hbm_connectivity,
    hbm_cell_scale,
    hbm_up_list,
    hbm_down_list,
    hbm_stiffness,
    hbm_rotation,
    out,
    orbitals,
    potential,
    connectivity,
    cell_scale,
    up_list,
    down_list,
    stiffness,
    rotation,
    pair_stiffness,
    one_hot,
    up_hot,
    down_hot,
    index_ref,
    scale_ref,
    index_turn,
    scale_turn,
    extended,
    sums,
    up_out,
    down_out,
    up_back,
    down_back,
    current,
    own_others,
    mate_others,
    own_filt,
    mate_filt,
    rotated,
    own_sem,
    others_send,
    others_recv,
    ghost_send,
    ghost_recv,
    back_send,
    back_recv,
    filt_send,
    filt_recv,
    out_sems,
    in_sems,
):
    rows, nodes = orbitals.shape
    rim = up_out.shape[2]
    ext_len = extended.shape[2]
    cells = connectivity.shape[1]
    groups = cells // GROUP
    low_end = 288 // GROUP
    high_start = groups - low_end
    low_half, high_half = low_end // 2, groups - low_end // 2
    low_cut = GROUP * low_half * (ext_len - WINDOW) // (cells - 1) // 128 * 128
    high_cut = GROUP * (high_half - 1) * (ext_len - WINDOW) // (cells - 1) // 128 * 128 + SPAN
    rest = others.shape[0]
    half = out.shape[0]
    piece = nodes // filt_send.shape[0]

    me = lax.axis_index("domain")
    band = lax.axis_index("band")
    above, below = lax.rem(me + 1, n_domain), lax.rem(me + n_domain - 1, n_domain)
    mate = 1 - band

    barrier = pltpu.get_barrier_semaphore()
    for target in ({"domain": above}, {"domain": below}, {"band": mate}):
        pl.semaphore_signal(barrier, inc=1, device_id=target, device_id_type=MESH)

    loads = []
    for k, (source, target) in enumerate(
        (
            (hbm_up_list, up_list),
            (hbm_orbitals, orbitals),
            (hbm_down_list, down_list),
            (hbm_connectivity, connectivity),
            (hbm_cell_scale, cell_scale),
            (hbm_stiffness, stiffness),
            (hbm_potential, potential),
            (hbm_rotation, rotation),
        )
    ):
        loads.append(pltpu.make_async_copy(source, target, in_sems.at[k]))
        loads[k].start()
    own_copy = pltpu.make_async_copy(others, own_others, own_sem)
    own_copy.start()
    loads[0].wait()
    list_one_hot(up_list, up_hot)
    loads[1].wait()
    loads[2].wait()
    list_one_hot(down_list, down_hot)

    def send_ghosts(source, step):
        pick(source, up_list, up_hot, up_out.at[step])
        up = pltpu.make_async_remote_copy(
            src_ref=up_out.at[step],
            dst_ref=extended.at[step, :, pl.ds(0, rim)],
            send_sem=ghost_send.at[step, 0],
            recv_sem=ghost_recv.at[step, 0],
            device_id={"domain": above},
            device_id_type=MESH,
        )
        if step == 0:
            pl.semaphore_wait(barrier, 3)
        up.start()
        pick(source, down_list, down_hot, down_out.at[step])
        down = pltpu.make_async_remote_copy(
            src_ref=down_out.at[step],
            dst_ref=extended.at[step, :, pl.ds(rim + nodes, rim)],
            send_sem=ghost_send.at[step, 1],
            recv_sem=ghost_recv.at[step, 1],
            device_id={"domain": below},
            device_id_type=MESH,
        )
        down.start()
        extended[step, :, rim : rim + nodes] = source[...]
        sums[step] = jnp.zeros((rows, ext_len), f32)
        return up, down

    def send_back(step, lower, part):
        edge = low_cut if lower else high_cut - rim - nodes
        first = 0 if (part == 0) == lower else edge
        count = edge if (part == 0) == lower else rim - edge
        sem = part if lower else 2 + part
        copy = pltpu.make_async_remote_copy(
            src_ref=sums.at[step, :, pl.ds(first if lower else rim + nodes + first, count)],
            dst_ref=(up_back if lower else down_back).at[step, :, pl.ds(first, count)],
            send_sem=back_send.at[step, sem],
            recv_sem=back_recv.at[step, sem],
            device_id={"domain": below if lower else above},
            device_id_type=MESH,
        )
        copy.start()
        return copy

    def lower_cells(step):
        cells_from(step, 0, low_half, 1, 9)
        first = send_back(step, True, 0)
        cells_from(step, low_half, low_end - low_half, 1, 9)
        return first, send_back(step, True, 1)

    def upper_cells(step):
        cells_from(step, groups - 1, groups - high_half, -1, 9)
        first = send_back(step, False, 0)
        cells_from(step, high_half - 1, high_half - high_start, -1, 9)
        return first, send_back(step, False, 1)

    def send_others(step):
        edges = (0, rest // 12 * 7, rest // 4 * 3, rest)
        cut = pl.ds(edges[step], edges[step + 1] - edges[step])
        copy = pltpu.make_async_remote_copy(
            src_ref=own_others.at[cut, :],
            dst_ref=mate_others.at[cut, :],
            send_sem=others_send.at[step],
            recv_sem=others_recv.at[step],
            device_id={"band": mate},
            device_id_type=MESH,
        )
        copy.start()
        return copy

    def cells_from(step, first, count, sign, unroll):
        run_cells(
            first,
            count,
            sign,
            unroll,
            extended.at[step],
            index_ref,
            scale_ref,
            pair_stiffness,
            one_hot,
            sums.at[step],
        )

    up, down = send_ghosts(orbitals, 0)
    for load in loads[3:]:
        load.wait()
    build_stiffness(stiffness, pair_stiffness)
    for k in range(cells // 128):
        cut = slice(128 * k, 128 * k + 128)
        pair_rows(connectivity[:, cut], index_turn, index_ref.at[64 * k : 64 * k + 64, :])
        pair_rows(
            jnp.broadcast_to(cell_scale[k : k + 1, :], (64, 128)), scale_turn, scale_ref.at[64 * k : 64 * k + 64, :]
        )
    build_cells(index_ref, one_hot, cells, ext_len)
    own_copy.wait()
    up.wait()
    down.wait()
    others_0 = send_others(0)
    lower = lower_cells(0)
    upper = upper_cells(0)
    cells_from(0, low_end, high_start - low_end, 1, 6)
    current[...] = sums[0, :, rim : rim + nodes]
    for copy in lower:
        copy.wait()
    place(up_back.at[0], up_list, up_hot, current)
    for copy in upper:
        copy.wait()
    others_1 = send_others(1)
    place(down_back.at[0], down_list, down_hot, current)
    for k in range(nodes // 256):
        cut = slice(256 * k, 256 * k + 256)
        before = orbitals[:, cut]
        current[:, cut] = (current[:, cut] + potential[:, cut] * before - CENTER * before) * (1.0 / HALF)

    up, down = send_ghosts(current, 1)
    cells_from(1, low_end, high_start - low_end, 1, 6)
    up.wait()
    others_2 = send_others(2)
    lower = lower_cells(1)
    down.wait()
    upper = upper_cells(1)
    own_filt[...] = sums[1, :, rim : rim + nodes]

    columns = pl.ds(pl.multiple_of(band * half, 128), half)

    def weights_of(first, count):
        return rotation[pl.ds(pl.multiple_of(first, 8), count), columns].T

    others_0.wait()
    others_1.wait()
    others_2.wait()
    high, low = split(
        jnp.concatenate([weights_of(2 * rows + rest * band, rest), weights_of(2 * rows + rest * mate, rest)], axis=1)
    )
    both_parts = jnp.concatenate([high, low], axis=0)

    def other_products(k, carry):
        cut = pl.ds(pl.multiple_of(256 * k, 256), 256)
        high_values, low_values = split(jnp.concatenate([own_others[:, cut], mate_others[:, cut]], axis=0))
        main = jnp.dot(both_parts, high_values, preferred_element_type=f32)
        rotated[:, cut] = main[:half] + main[half:] + jnp.dot(high, low_values, preferred_element_type=f32)
        return carry

    lax.fori_loop(0, nodes // 256, other_products, 0, unroll=2)
    own_weights = pieces(weights_of(rows * band, rows))
    mate_weights = pieces(weights_of(rows * mate, rows))

    for copy in lower:
        copy.wait()
    place(up_back.at[1], up_list, up_hot, own_filt)
    for copy in upper:
        copy.wait()
    place(down_back.at[1], down_list, down_hot, own_filt)
    copies = []
    for k in range(nodes // piece):
        cut = slice(piece * k, piece * k + piece)
        now = current[:, cut]
        own_filt[:, cut] = (own_filt[:, cut] + potential[:, cut] * now - CENTER * now) * (2.0 / HALF) - orbitals[:, cut]
        copy = pltpu.make_async_remote_copy(
            src_ref=own_filt.at[:, pl.ds(piece * k, piece)],
            dst_ref=mate_filt.at[:, pl.ds(piece * k, piece)],
            send_sem=filt_send.at[k],
            recv_sem=filt_recv.at[k],
            device_id={"band": mate},
            device_id_type=MESH,
        )
        copy.start()
        copies.append(copy)
    for k in range(nodes // 256):
        cut = slice(256 * k, 256 * k + 256)
        rotated[:, cut] += times(own_weights, own_filt[:, cut])
    writes = []
    for k in range(nodes // piece):
        copies[k].wait()
        for j in range(piece // 256):
            cut = slice(piece * k + 256 * j, piece * k + 256 * j + 256)
            rotated[:, cut] += times(mate_weights, mate_filt[:, cut])
        write = pltpu.make_async_copy(
            rotated.at[:, pl.ds(piece * k, piece)], out.at[:, pl.ds(piece * k, piece)], out_sems.at[k]
        )
        write.start()
        writes.append(write)
    for write in writes:
        write.wait()


def body(
    orbitals, others, potential, cell_scale, connectivity, send_up, send_down, stiffness, rotation
):
    rows, nodes = orbitals.shape
    rest = others.shape[0]
    rim = send_up.shape[0]
    npc, cells = connectivity.shape
    ext_len = nodes + 2 * rim
    panel = rotation.shape[0]
    half = panel // lax.axis_size("band")
    parts = 4
    hbm = pl.BlockSpec(memory_space=pl.ANY)
    return pl.pallas_call(
        functools.partial(kernel, lax.axis_size("domain")),
        out_shape=jax.ShapeDtypeStruct((half, nodes), f32),
        in_specs=[hbm] * 9,
        out_specs=hbm,
        scratch_shapes=[
            pltpu.VMEM((rows, nodes), f32),
            pltpu.VMEM((1, nodes), f32),
            pltpu.VMEM((npc, cells), jnp.int32),
            pltpu.VMEM((cells // 128, 128), f32),
            pltpu.VMEM((rim // 128, 128), jnp.int32),
            pltpu.VMEM((rim // 128, 128), jnp.int32),
            pltpu.VMEM((npc, npc), f32),
            pltpu.VMEM((panel, panel), f32),
            pltpu.VMEM((4 * npc, 4 * npc), bf16),
            pltpu.VMEM((cells // GROUP, GROUP * npc, 256), bf16),
            pltpu.VMEM((256, rim), bf16),
            pltpu.VMEM((256, rim), bf16),
            pltpu.VMEM((cells // 2, 2 * npc), jnp.int32),
            pltpu.VMEM((cells // 2, 2 * npc), f32),
            pltpu.VMEM((128, 128), jnp.int32),
            pltpu.VMEM((128, 128), f32),
            pltpu.VMEM((2, rows, ext_len), f32),
            pltpu.VMEM((2, rows, ext_len), f32),
            pltpu.VMEM((2, rows, rim), f32),
            pltpu.VMEM((2, rows, rim), f32),
            pltpu.VMEM((2, rows, rim), f32),
            pltpu.VMEM((2, rows, rim), f32),
            pltpu.VMEM((rows, nodes), f32),
            pltpu.VMEM((rest, nodes), f32),
            pltpu.VMEM((rest, nodes), f32),
            pltpu.VMEM((rows, nodes), f32),
            pltpu.VMEM((rows, nodes), f32),
            pltpu.VMEM((half, nodes), f32),
            pltpu.SemaphoreType.DMA,
            pltpu.SemaphoreType.DMA((3,)),
            pltpu.SemaphoreType.DMA((3,)),
            pltpu.SemaphoreType.DMA((2, 2)),
            pltpu.SemaphoreType.DMA((2, 2)),
            pltpu.SemaphoreType.DMA((2, 4)),
            pltpu.SemaphoreType.DMA((2, 4)),
            pltpu.SemaphoreType.DMA((parts,)),
            pltpu.SemaphoreType.DMA((parts,)),
            pltpu.SemaphoreType.DMA((parts,)),
            pltpu.SemaphoreType.DMA((8,)),
        ],
        compiler_params=pltpu.CompilerParams(
            collective_id=0, has_side_effects=True, vmem_limit_bytes=64 * 2**20
        ),
        name="filter_rotate",
    )(
        orbitals,
        others,
        potential.reshape(1, nodes),
        connectivity,
        cell_scale.reshape(cells // 128, 128),
        send_up.reshape(rim // 128, 128),
        send_down.reshape(rim // 128, 128),
        stiffness,
        rotation,
    )


def solution(mesh):
    placed = (
        P("band", "domain"),
        P("band", "domain"),
        P("domain"),
        P("domain"),
        P(None, "domain"),
        P("domain"),
        P("domain"),
        P(),
        P(),
    )
    return jax.shard_map(
        body, mesh=mesh, in_specs=placed, out_specs=P("band", "domain"), check_vma=False
    )
```

```python
import functools

import jax
import jax.numpy as jnp
from jax import lax
from jax.experimental import pallas as pl
from jax.experimental.pallas import tpu as pltpu
from jax.sharding import PartitionSpec as P

bf16 = jnp.bfloat16
f32 = jnp.float32
MESH = pl.DeviceIdType.MESH

WINDOW = 256
CENTER = 64.0
HALF = 64.0

GROUP = 16
PAIRS = GROUP // 2
SPAN = 512


def split(values):
    high = values.astype(bf16)
    return high, (values - high.astype(f32)).astype(bf16)


def group_base(g, cells, ext_len):
    first = (GROUP * g * (ext_len - WINDOW)) // (cells - 1)
    return pl.multiple_of(jnp.minimum((first // 128) * 128, ext_len - SPAN), 128)


def list_one_hot(list_ref, one_hot):
    lanes = lax.broadcasted_iota(jnp.int32, (256, 128), 0)
    for j in range(list_ref.shape[0]):
        entry = jnp.broadcast_to(list_ref[j : j + 1, :] & 255, (256, 128))
        one_hot[:, 128 * j : 128 * j + 128] = jnp.where(lanes == entry, 1.0, 0.0).astype(bf16)


def pick(source, list_ref, one_hot, target):
    rows, nodes = source.shape
    blocks = nodes // 256
    parts = [split(source[:, 256 * k : 256 * k + 256]) for k in range(blocks)]
    left = jnp.concatenate([p[0] for p in parts] + [p[1] for p in parts], axis=0)
    for j in range(list_ref.shape[0] // 2):
        both = jnp.dot(left, one_hot[:, 256 * j : 256 * j + 256], preferred_element_type=f32)
        block = jnp.concatenate([list_ref[2 * j : 2 * j + 1, :], list_ref[2 * j + 1 : 2 * j + 2, :]], axis=1) >> 8
        block = jnp.broadcast_to(block, (rows, 256))
        total = jnp.zeros((rows, 256), f32)
        for k in range(blocks):
            here = both[rows * k : rows * k + rows] + both[rows * (blocks + k) : rows * (blocks + k) + rows]
            total = jnp.where(block == k, here, total)
        target[:, 256 * j : 256 * j + 256] = total


def place(source, list_ref, one_hot, target):
    rows, nodes = target.shape
    blocks = nodes // 256
    entries = source.shape[1]
    columns = []
    for j in range(entries // 128):
        high, low = split(source[:, 128 * j : 128 * j + 128])
        block = (list_ref[j : j + 1, :] >> 8).astype(f32).astype(bf16)
        block = jnp.broadcast_to(block, (rows, 128))
        zero = jnp.zeros_like(high)
        masks = [block == k for k in range(blocks)]
        columns.append(
            jnp.concatenate(
                [jnp.where(m, high, zero) for m in masks] + [jnp.where(m, low, zero) for m in masks], axis=0
            )
        )
    left = jnp.concatenate(columns, axis=1)
    both = lax.dot_general(left, one_hot[...], (((1,), (1,)), ((), ())), preferred_element_type=f32)
    for k in range(blocks):
        here = both[rows * k : rows * k + rows] + both[rows * (blocks + k) : rows * (blocks + k) + rows]
        target[:, 256 * k : 256 * k + 256] += here


def build_stiffness(stiffness, paired):
    high, low = split(stiffness[...])
    none = jnp.zeros_like(high)
    rows = [[high, none, low, none], [none, high, none, low], [high, none, none, none], [none, high, none, none]]
    paired[...] = jnp.concatenate([jnp.concatenate(row, axis=1) for row in rows], axis=0)


def build_cells(index_ref, one_hot, cells, ext_len):
    def step(g, carry):
        base = group_base(g, cells, ext_len)
        local = (index_ref[pl.ds(pl.multiple_of(PAIRS * g, PAIRS), PAIRS), :] - base) & 255
        local = local.astype(f32).astype(bf16)
        lanes = lax.broadcasted_iota(jnp.int32, (128, 256), 1).astype(f32).astype(bf16)
        one, zero = jnp.ones((128, 256), bf16), jnp.zeros((128, 256), bf16)
        for h in range(PAIRS):
            entry = jnp.broadcast_to(local[h : h + 1, :], (128, 128)).T
            entry = jnp.concatenate([entry, entry], axis=1)
            one_hot[g, 128 * h : 128 * h + 128, :] = jnp.where(lanes == entry, one, zero)
        return carry

    lax.fori_loop(0, cells // GROUP, step, 0, unroll=4)


def run_cells(first, count, sign, unroll, extended, index_ref, scale_ref, pair_stiffness, one_hot, summed):
    rows, ext_len = extended.shape
    cells = 2 * index_ref.shape[0]
    row_tiles = rows // 8

    def step(i, carry):
        g = first + sign * i
        base = group_base(g, cells, ext_len)
        source = [
            [extended[8 * o : 8 * o + 8, pl.ds(base + 128 * k, 128)] for k in range(4)] for o in range(row_tiles)
        ]
        at = pl.multiple_of(PAIRS * g, PAIRS)
        local = index_ref[pl.ds(at, PAIRS), :] - base
        scales = scale_ref[pl.ds(at, PAIRS), :]
        values, upper = [], []
        for h in range(PAIRS):
            position = jnp.broadcast_to(local[h : h + 1, :], (8, 128))
            block, lane = position >> 7, position & 127
            tiles = []
            for o in range(row_tiles):
                tile = jnp.take_along_axis(source[o][0], lane, axis=1)
                for k in range(1, 4):
                    tile = jnp.where(block == k, jnp.take_along_axis(source[o][k], lane, axis=1), tile)
                tiles.append(tile)
            values.append(jnp.concatenate(split(jnp.concatenate(tiles, axis=0)), axis=1))
            upper.append(jnp.concatenate([block] * row_tiles, axis=0) >= 2)
        images = jnp.dot(jnp.concatenate(values, axis=0), pair_stiffness[...], preferred_element_type=f32)
        images = images[:, :128] + images[:, 128:]
        columns = []
        for h in range(PAIRS):
            image = images[rows * h : rows * h + rows] * jnp.broadcast_to(scales[h : h + 1, :], (rows, 128))
            high = image.astype(bf16).astype(f32)
            low = image - high
            zero = jnp.zeros_like(image)
            columns.append(
                jnp.concatenate(
                    [
                        jnp.where(upper[h], zero, high),
                        jnp.where(upper[h], high, zero),
                        jnp.where(upper[h], zero, low),
                        jnp.where(upper[h], low, zero),
                    ],
                    axis=0,
                ).astype(bf16)
            )
        left = jnp.concatenate(columns, axis=1)
        both = jnp.dot(left, one_hot[g], preferred_element_type=f32)
        added = both[: 2 * rows] + both[2 * rows :]
        summed[:, pl.ds(base, 256)] += added[:rows]
        summed[:, pl.ds(base + 256, 256)] += added[rows:]
        return carry

    lax.fori_loop(0, count, step, 0, unroll=unroll)


def pair_rows(block, turn, target):
    turn[...] = jnp.concatenate([block, pltpu.roll(block, 127, 1)], axis=0).T
    target[...] = turn[pl.ds(0, 64, stride=2), :]


def pieces(weights):
    high, low = split(weights)
    return jnp.concatenate([high, high, low], axis=1)


def times(weights, values):
    high, low = split(values)
    return jnp.dot(weights, jnp.concatenate([high, low, high], axis=0), preferred_element_type=f32)


def kernel(
    n_domain,
    hbm_orbitals,
    others,
    hbm_potential,
    hbm_connectivity,
    hbm_cell_scale,
    hbm_up_list,
    hbm_down_list,
    hbm_stiffness,
    hbm_rotation,
    out_top,
    out_rest,
    orbitals,
    potential,
    connectivity,
    cell_scale,
    up_list,
    down_list,
    stiffness,
    rotation,
    pair_stiffness,
    one_hot,
    up_hot,
    down_hot,
    index_ref,
    scale_ref,
    index_turn,
    scale_turn,
    extended,
    sums,
    up_out,
    down_out,
    up_back,
    down_back,
    current,
    own_others,
    mate_others,
    own_filt,
    mate_filt,
    rotated,
    own_sem,
    others_send,
    others_recv,
    ghost_send,
    ghost_recv,
    back_send,
    back_recv,
    filt_send,
    filt_recv,
    out_sems,
    in_sems,
):
    rows, nodes = orbitals.shape
    rim = up_out.shape[2]
    ext_len = extended.shape[2]
    cells = connectivity.shape[1]
    groups = cells // GROUP
    low_end = 288 // GROUP
    high_start = groups - low_end
    low_half, high_half = low_end // 2, groups - low_end // 2
    low_cut = GROUP * low_half * (ext_len - WINDOW) // (cells - 1) // 128 * 128
    high_cut = GROUP * (high_half - 1) * (ext_len - WINDOW) // (cells - 1) // 128 * 128 + SPAN
    rest = others.shape[0]
    top = out_top.shape[0]
    half = top + out_rest.shape[0]
    piece = nodes // filt_send.shape[0]

    me = lax.axis_index("domain")
    band = lax.axis_index("band")
    above, below = lax.rem(me + 1, n_domain), lax.rem(me + n_domain - 1, n_domain)
    mate = 1 - band

    barrier = pltpu.get_barrier_semaphore()
    for target in ({"domain": above}, {"domain": below}, {"band": mate}):
        pl.semaphore_signal(barrier, inc=1, device_id=target, device_id_type=MESH)

    loads = []
    for k, (source, target) in enumerate(
        (
            (hbm_up_list, up_list),
            (hbm_orbitals, orbitals),
            (hbm_down_list, down_list),
            (hbm_connectivity, connectivity),
            (hbm_cell_scale, cell_scale),
            (hbm_stiffness, stiffness),
            (hbm_potential, potential),
            (hbm_rotation, rotation),
        )
    ):
        loads.append(pltpu.make_async_copy(source, target, in_sems.at[k]))
        loads[k].start()
    own_copy = pltpu.make_async_copy(others, own_others, own_sem)
    own_copy.start()
    loads[0].wait()
    list_one_hot(up_list, up_hot)
    loads[1].wait()
    loads[2].wait()
    list_one_hot(down_list, down_hot)

    def send_ghosts(source, step):
        pick(source, up_list, up_hot, up_out.at[step])
        up = pltpu.make_async_remote_copy(
            src_ref=up_out.at[step],
            dst_ref=extended.at[step, :, pl.ds(0, rim)],
            send_sem=ghost_send.at[step, 0],
            recv_sem=ghost_recv.at[step, 0],
            device_id={"domain": above},
            device_id_type=MESH,
        )
        if step == 0:
            pl.semaphore_wait(barrier, 3)
        up.start()
        pick(source, down_list, down_hot, down_out.at[step])
        down = pltpu.make_async_remote_copy(
            src_ref=down_out.at[step],
            dst_ref=extended.at[step, :, pl.ds(rim + nodes, rim)],
            send_sem=ghost_send.at[step, 1],
            recv_sem=ghost_recv.at[step, 1],
            device_id={"domain": below},
            device_id_type=MESH,
        )
        down.start()
        extended[step, :, rim : rim + nodes] = source[...]
        sums[step] = jnp.zeros((rows, ext_len), f32)
        return up, down

    def send_back(step, lower, part):
        edge = low_cut if lower else high_cut - rim - nodes
        first = 0 if (part == 0) == lower else edge
        count = edge if (part == 0) == lower else rim - edge
        sem = part if lower else 2 + part
        copy = pltpu.make_async_remote_copy(
            src_ref=sums.at[step, :, pl.ds(first if lower else rim + nodes + first, count)],
            dst_ref=(up_back if lower else down_back).at[step, :, pl.ds(first, count)],
            send_sem=back_send.at[step, sem],
            recv_sem=back_recv.at[step, sem],
            device_id={"domain": below if lower else above},
            device_id_type=MESH,
        )
        copy.start()
        return copy

    def lower_cells(step):
        cells_from(step, 0, low_half, 1, 9)
        first = send_back(step, True, 0)
        cells_from(step, low_half, low_end - low_half, 1, 9)
        return first, send_back(step, True, 1)

    def upper_cells(step):
        cells_from(step, groups - 1, groups - high_half, -1, 9)
        first = send_back(step, False, 0)
        cells_from(step, high_half - 1, high_half - high_start, -1, 9)
        return first, send_back(step, False, 1)

    def send_others(step):
        edges = (0, rest // 12 * 7, rest // 4 * 3, rest)
        cut = pl.ds(edges[step], edges[step + 1] - edges[step])
        copy = pltpu.make_async_remote_copy(
            src_ref=own_others.at[cut, :],
            dst_ref=mate_others.at[cut, :],
            send_sem=others_send.at[step],
            recv_sem=others_recv.at[step],
            device_id={"band": mate},
            device_id_type=MESH,
        )
        copy.start()
        return copy

    def cells_from(step, first, count, sign, unroll):
        run_cells(
            first,
            count,
            sign,
            unroll,
            extended.at[step],
            index_ref,
            scale_ref,
            pair_stiffness,
            one_hot,
            sums.at[step],
        )

    up, down = send_ghosts(orbitals, 0)
    for load in loads[3:]:
        load.wait()
    build_stiffness(stiffness, pair_stiffness)
    for k in range(cells // 128):
        cut = slice(128 * k, 128 * k + 128)
        pair_rows(connectivity[:, cut], index_turn, index_ref.at[64 * k : 64 * k + 64, :])
        pair_rows(
            jnp.broadcast_to(cell_scale[k : k + 1, :], (64, 128)), scale_turn, scale_ref.at[64 * k : 64 * k + 64, :]
        )
    build_cells(index_ref, one_hot, cells, ext_len)
    own_copy.wait()
    up.wait()
    down.wait()
    others_0 = send_others(0)
    lower = lower_cells(0)
    upper = upper_cells(0)
    cells_from(0, low_end, high_start - low_end, 1, 6)
    current[...] = sums[0, :, rim : rim + nodes]
    for copy in lower:
        copy.wait()
    place(up_back.at[0], up_list, up_hot, current)
    for copy in upper:
        copy.wait()
    others_1 = send_others(1)
    place(down_back.at[0], down_list, down_hot, current)
    for k in range(nodes // 256):
        cut = slice(256 * k, 256 * k + 256)
        before = orbitals[:, cut]
        current[:, cut] = (current[:, cut] + potential[:, cut] * before - CENTER * before) * (1.0 / HALF)

    up, down = send_ghosts(current, 1)
    cells_from(1, low_end, high_start - low_end, 1, 6)
    up.wait()
    others_2 = send_others(2)
    lower = lower_cells(1)
    down.wait()
    upper = upper_cells(1)
    own_filt[...] = sums[1, :, rim : rim + nodes]

    columns = pl.ds(pl.multiple_of(band * half, 128), half)

    def weights_of(first, count):
        return rotation[pl.ds(pl.multiple_of(first, 8), count), columns].T

    others_0.wait()
    others_1.wait()
    others_2.wait()
    high, low = split(
        jnp.concatenate([weights_of(2 * rows + rest * band, rest), weights_of(2 * rows + rest * mate, rest)], axis=1)
    )
    both_parts = jnp.concatenate([high, low], axis=0)

    def other_products(k, carry):
        cut = pl.ds(pl.multiple_of(256 * k, 256), 256)
        high_values, low_values = split(jnp.concatenate([own_others[:, cut], mate_others[:, cut]], axis=0))
        main = jnp.dot(both_parts, high_values, preferred_element_type=f32)
        rotated[:, cut] = main[:half] + main[half:] + jnp.dot(high, low_values, preferred_element_type=f32)
        return carry

    lax.fori_loop(0, nodes // 256, other_products, 0, unroll=2)
    own_weights = pieces(weights_of(rows * band, rows))
    mate_weights = pieces(weights_of(rows * mate, rows))

    for copy in lower:
        copy.wait()
    place(up_back.at[1], up_list, up_hot, own_filt)
    for copy in upper:
        copy.wait()
    place(down_back.at[1], down_list, down_hot, own_filt)
    copies = []
    for k in range(nodes // piece):
        cut = slice(piece * k, piece * k + piece)
        now = current[:, cut]
        own_filt[:, cut] = (own_filt[:, cut] + potential[:, cut] * now - CENTER * now) * (2.0 / HALF) - orbitals[:, cut]
        copy = pltpu.make_async_remote_copy(
            src_ref=own_filt.at[:, pl.ds(piece * k, piece)],
            dst_ref=mate_filt.at[:, pl.ds(piece * k, piece)],
            send_sem=filt_send.at[k],
            recv_sem=filt_recv.at[k],
            device_id={"band": mate},
            device_id_type=MESH,
        )
        copy.start()
        copies.append(copy)
    for k in range(nodes // 256):
        cut = slice(256 * k, 256 * k + 256)
        rotated[:, cut] += times(own_weights, own_filt[:, cut])
    writes = []
    for k in range(nodes // piece):
        copies[k].wait()
        for j in range(piece // 256):
            cut = slice(piece * k + 256 * j, piece * k + 256 * j + 256)
            rotated[:, cut] += times(mate_weights, mate_filt[:, cut])
        cut = pl.ds(piece * k, piece)
        for j, (target, first, count) in enumerate(((out_top, 0, top), (out_rest, top, half - top))):
            write = pltpu.make_async_copy(rotated.at[pl.ds(first, count), cut], target.at[:, cut], out_sems.at[j, k])
            write.start()
            writes.append(write)
    for write in writes:
        write.wait()


def body(
    orbitals, others, potential, cell_scale, connectivity, send_up, send_down, stiffness, rotation
):
    rows, nodes = orbitals.shape
    rest = others.shape[0]
    rim = send_up.shape[0]
    npc, cells = connectivity.shape
    ext_len = nodes + 2 * rim
    panel = rotation.shape[0]
    half = panel // lax.axis_size("band")
    parts = 4
    hbm = pl.BlockSpec(memory_space=pl.ANY)
    halves = pl.pallas_call(
        functools.partial(kernel, lax.axis_size("domain")),
        out_shape=[jax.ShapeDtypeStruct((half // 2, nodes), f32)] * 2,
        in_specs=[hbm] * 9,
        out_specs=[hbm] * 2,
        scratch_shapes=[
            pltpu.VMEM((rows, nodes), f32),
            pltpu.VMEM((1, nodes), f32),
            pltpu.VMEM((npc, cells), jnp.int32),
            pltpu.VMEM((cells // 128, 128), f32),
            pltpu.VMEM((rim // 128, 128), jnp.int32),
            pltpu.VMEM((rim // 128, 128), jnp.int32),
            pltpu.VMEM((npc, npc), f32),
            pltpu.VMEM((panel, panel), f32),
            pltpu.VMEM((4 * npc, 4 * npc), bf16),
            pltpu.VMEM((cells // GROUP, GROUP * npc, 256), bf16),
            pltpu.VMEM((256, rim), bf16),
            pltpu.VMEM((256, rim), bf16),
            pltpu.VMEM((cells // 2, 2 * npc), jnp.int32),
            pltpu.VMEM((cells // 2, 2 * npc), f32),
            pltpu.VMEM((128, 128), jnp.int32),
            pltpu.VMEM((128, 128), f32),
            pltpu.VMEM((2, rows, ext_len), f32),
            pltpu.VMEM((2, rows, ext_len), f32),
            pltpu.VMEM((2, rows, rim), f32),
            pltpu.VMEM((2, rows, rim), f32),
            pltpu.VMEM((2, rows, rim), f32),
            pltpu.VMEM((2, rows, rim), f32),
            pltpu.VMEM((rows, nodes), f32),
            pltpu.VMEM((rest, nodes), f32),
            pltpu.VMEM((rest, nodes), f32),
            pltpu.VMEM((rows, nodes), f32),
            pltpu.VMEM((rows, nodes), f32),
            pltpu.VMEM((half, nodes), f32),
            pltpu.SemaphoreType.DMA,
            pltpu.SemaphoreType.DMA((3,)),
            pltpu.SemaphoreType.DMA((3,)),
            pltpu.SemaphoreType.DMA((2, 2)),
            pltpu.SemaphoreType.DMA((2, 2)),
            pltpu.SemaphoreType.DMA((2, 4)),
            pltpu.SemaphoreType.DMA((2, 4)),
            pltpu.SemaphoreType.DMA((parts,)),
            pltpu.SemaphoreType.DMA((parts,)),
            pltpu.SemaphoreType.DMA((2, parts)),
            pltpu.SemaphoreType.DMA((8,)),
        ],
        compiler_params=pltpu.CompilerParams(
            collective_id=0, has_side_effects=True, vmem_limit_bytes=64 * 2**20
        ),
        name="filter_rotate",
    )(
        orbitals,
        others,
        potential.reshape(1, nodes),
        connectivity,
        cell_scale.reshape(cells // 128, 128),
        send_up.reshape(rim // 128, 128),
        send_down.reshape(rim // 128, 128),
        stiffness,
        rotation,
    )
    return jnp.concatenate(halves, axis=0)


def solution(mesh):
    placed = (
        P("band", "domain"),
        P("band", "domain"),
        P("domain"),
        P("domain"),
        P(None, "domain"),
        P("domain"),
        P("domain"),
        P(),
        P(),
    )
    return jax.shard_map(
        body, mesh=mesh, in_specs=placed, out_specs=P("band", "domain"), check_vma=False
    )
```
